32 devices in a mesh: lat: 8 (over y, x, core), lon: 4 (over z).
Axes of the slice: x: 2, y: 2, z: 4, core: 2. Of those that a mesh axis runs over, the one named last changes fastest.
Arguments:
- query_field: bfloat16 [64, 64, 512], P('lat', 'lon'), may hold values from -6 to 6
- key_field: bfloat16 [64, 64, 512], P('lat', 'lon'), may hold values from -6 to 6
- value_field: bfloat16 [64, 64, 512], P('lat', 'lon'), may hold values from -6 to 6
- out_grad: bfloat16 [64, 64, 512], P('lat', 'lon'), may hold values from -24 to 24
- pole_reach: int32 [2, 64], replicated, may hold values from 0 to 6
Outputs:
- query_grad: bfloat16 [64, 64, 512], P('lat', 'lon')
- key_grad: bfloat16 [64, 64, 512], P('lat', 'lon')
- value_grad: bfloat16 [64, 64, 512], P('lat', 'lon')
The draws below stay inside these ranges and needn't reach their ends.
All inputs are finite; a program needn't handle non-finite values.
Results may differ from the reference program's by a relative error of at most 0.012.
The reference program's roundings to bfloat16 on the way (of `probs_half` and `grad_scores`) count: a program that leaves them out, or rounds other values in their place, can miss the bound.
Values may be sent and summed in bfloat16 or wider, within the bound.
No kernel may reach another device: no remote copies, remote signals or barrier semaphores. Data moves between devices by JAX's collectives and lax.ppermute only.
A program may use at most 64 MiB of HBM per device.

```python
import math
import jax
import jax.numpy as jnp
from jax import lax

HEADS = 16
HEAD_DIM = 32
RADIUS = 6
BAND_ROWS = 8
SECTOR_COLS = 16
D = 512
ROWS = 64
COLS = 64
N_LAT = 8
N_LON = 4


def draw_query_field(key, part):
    field = jnp.clip(jax.random.normal(jax.random.fold_in(key, 1), (ROWS, COLS, D)), -6.0, 6.0)
    return field.astype(jnp.float32).astype(jnp.bfloat16)


def draw_key_field(key, part):
    field = jnp.clip(jax.random.normal(jax.random.fold_in(key, 2), (ROWS, COLS, D)), -6.0, 6.0)
    return field.astype(jnp.float32).astype(jnp.bfloat16)


def with_ends(entries, rng, low, high):
    dims = entries.shape
    spot = [jax.random.randint(jax.random.fold_in(rng, axis), (), 0, dims[axis]) for axis in range(len(dims))]
    entries = entries.at[tuple(spot)].set(low)
    longest = dims.index(max(dims))
    spot[longest] = (spot[longest] + 1) % dims[longest]
    return entries.at[tuple(spot)].set(high)


def block_scale(key, shape, pieces, low, top_value):
    level, own = 1.0, jax.random.fold_in(key, 6)
    for dim, shards_of in pieces:
        draws = jnp.exp(jax.random.uniform(jax.random.fold_in(own, dim), (shards_of,), jnp.float32, low / len(pieces), top_value / len(pieces)))
        level = level * jnp.repeat(draws, shape[dim] // shards_of).reshape([-1 if axis == dim else 1 for axis in range(len(shape))])
    return level


def normal_values(stream_key, dims, width, bound, pieces=(), kind=jnp.bfloat16):
    result = width * jax.random.normal(stream_key, dims, jnp.float32)
    if pieces:
        result = result * block_scale(stream_key, dims, pieces, -0.22, 0.18)
    return jnp.clip(result, -bound, bound).astype(kind)


def setup_inputs(seed: int = 0) -> dict:
    splits = jax.random.split(jax.random.key(seed), 6)
    return {
        "query_field": draw_query_field(jax.random.fold_in(splits[5], 71), 0),
        "key_field": draw_key_field(jax.random.fold_in(splits[5], 71), 0),
        "value_field": normal_values(splits[2], (ROWS, COLS, D), 1.0, 6.0, ((0, 8), (1, 4))),
        "out_grad": normal_values(splits[3], (ROWS, COLS, D), 4.0, 24.0, ((0, 8), (1, 4))),
        "pole_reach": with_ends(jax.random.randint(splits[4], (2, COLS), 0, RADIUS + 1), jax.random.fold_in(splits[4], 1), 0, RADIUS).astype(jnp.int32),
    }


def lookup_row(table_row, positions, extent):
    match = positions[:, None] == jnp.arange(extent, dtype=jnp.int32)[None, :]
    return lax.optimization_barrier(jnp.sum(jnp.where(match, table_row[None, :], 0), axis=1))

def neighbour_mask(pole_reach, lat_index, lon_index, block_rows, block_cols, total_rows, total_cols):
    local_rows = jnp.arange(block_rows, dtype=jnp.int32)
    local_cols = jnp.arange(block_cols, dtype=jnp.int32)
    outer_rows = jnp.arange(block_rows + 2 * RADIUS, dtype=jnp.int32)
    outer_cols = jnp.arange(block_cols + 2 * RADIUS, dtype=jnp.int32)
    global_rows = lat_index * block_rows + local_rows
    global_cols = lon_index * block_cols + local_cols
    padded_rows = lat_index * block_rows + outer_rows
    key_cols = jnp.remainder(lon_index * block_cols + outer_cols - RADIUS + total_cols // 2, total_cols)
    north_band = padded_rows < RADIUS
    south_band = padded_rows >= total_rows + RADIUS
    north_depth = RADIUS - 1 - padded_rows
    south_depth = padded_rows - total_rows - RADIUS
    north_key = lookup_row(pole_reach[0], key_cols, total_cols)
    south_key = lookup_row(pole_reach[1], key_cols, total_cols)
    key_valid = jnp.where(north_band[:, None], north_key[None, :] > north_depth[:, None], jnp.where(south_band[:, None], south_key[None, :] > south_depth[:, None], True))
    north_query = lookup_row(pole_reach[0], global_cols, total_cols)[None, :] > global_rows[:, None]
    south_query = lookup_row(pole_reach[1], global_cols, total_cols)[None, :] > (total_rows - 1 - global_rows)[:, None]
    row_near = (outer_rows[None, :] >= local_rows[:, None]) & (outer_rows[None, :] <= local_rows[:, None] + 2 * RADIUS)
    col_near = (outer_cols[None, :] >= local_cols[:, None]) & (outer_cols[None, :] <= local_cols[:, None] + 2 * RADIUS)
    allowed = row_near[:, None, :, None] & col_near[None, :, None, :] & key_valid[None, None, :, :]
    allowed = allowed & (jnp.logical_not(north_band)[None, None, :, None] | north_query[:, :, None, None])
    allowed = allowed & (jnp.logical_not(south_band)[None, None, :, None] | south_query[:, :, None, None])
    return allowed.reshape(block_rows * block_cols, -1)

def pad_global(field):
    half_turn = COLS // 2
    north = jnp.flip(jnp.roll(field[:RADIUS], -half_turn, axis=1), axis=0)
    south = jnp.flip(jnp.roll(field[ROWS - RADIUS:], -half_turn, axis=1), axis=0)
    tall = jnp.concatenate([north, field, south], axis=0)
    return jnp.concatenate([tall[:, COLS - RADIUS:], tall, tall[:, :RADIUS]], axis=1)

def split_heads(field):
    return field.reshape(field.shape[0], HEADS, HEAD_DIM).astype(jnp.float32)

def query_block(query_rows, key_rows, value_rows, grad_rows, allowed):
    scale = 1.0 / math.sqrt(HEAD_DIM)
    query_heads = split_heads(query_rows)
    key_heads = split_heads(key_rows)
    value_heads = split_heads(value_rows)
    grad_heads = split_heads(grad_rows)
    scores = jnp.einsum('qhd,khd->hqk', query_heads, key_heads) * scale
    masked = jnp.where(allowed[None], scores, -1e+30)
    row_max = lax.optimization_barrier(jnp.max(masked, axis=2, keepdims=True))
    row_total = lax.optimization_barrier(jnp.sum(jnp.where(allowed[None], jnp.exp(masked - row_max), 0.0), axis=2, keepdims=True))
    log_total = row_max + jnp.log(row_total)
    probs = jnp.where(allowed[None], jnp.exp(scores - log_total), 0.0)
    probs_half = probs.astype(jnp.bfloat16).astype(jnp.float32)
    attended = jnp.einsum('hqk,khd->qhd', probs_half, value_heads)
    grad_dot = lax.optimization_barrier(jnp.sum(grad_heads * attended, axis=2))
    grad_probs = jnp.einsum('qhd,khd->hqk', grad_heads, value_heads)
    grad_scores = (probs * (grad_probs - grad_dot.T[:, :, None])).astype(jnp.bfloat16).astype(jnp.float32)
    query_grad = (jnp.einsum('hqk,khd->qhd', grad_scores, key_heads) * scale).astype(jnp.bfloat16)
    return (log_total[:, :, 0].T, grad_dot, query_grad.reshape(query_rows.shape[0], -1))

def key_block(key_rows, value_rows, query_outer, grad_outer, log_outer, dot_outer, allowed):
    scale = 1.0 / math.sqrt(HEAD_DIM)
    key_heads = split_heads(key_rows)
    value_heads = split_heads(value_rows)
    query_heads = split_heads(query_outer)
    grad_heads = split_heads(grad_outer)
    scores = jnp.einsum('khd,qhd->hkq', key_heads, query_heads) * scale
    probs = jnp.where(allowed[None], jnp.exp(scores - log_outer.T[:, None, :]), 0.0)
    probs_half = probs.astype(jnp.bfloat16).astype(jnp.float32)
    value_grad = jnp.einsum('hkq,qhd->khd', probs_half, grad_heads).astype(jnp.bfloat16)
    grad_probs = jnp.einsum('khd,qhd->hkq', value_heads, grad_heads)
    grad_scores = (probs * (grad_probs - dot_outer.T[:, None, :])).astype(jnp.bfloat16).astype(jnp.float32)
    key_grad = (jnp.einsum('hkq,qhd->khd', grad_scores, query_heads) * scale).astype(jnp.bfloat16)
    return (key_grad.reshape(key_rows.shape[0], -1), value_grad.reshape(key_rows.shape[0], -1))

def to_grid(stacked):
    depth = stacked.shape[-1]
    shaped = stacked.reshape(N_LAT, N_LON, BAND_ROWS, SECTOR_COLS, depth)
    return shaped.transpose(0, 2, 1, 3, 4).reshape(ROWS, COLS, depth)

def reference(query_field, key_field, value_field, out_grad, pole_reach):
    padded_query = pad_global(query_field)
    padded_key = pad_global(key_field)
    padded_value = pad_global(value_field)
    padded_grad = pad_global(out_grad)
    outer_shape = (BAND_ROWS + 2 * RADIUS, SECTOR_COLS + 2 * RADIUS)

    def cut_outer(padded, lat_index, lon_index):
        start = (lat_index * BAND_ROWS, lon_index * SECTOR_COLS, lat_index * 0)
        piece = lax.dynamic_slice(padded, start, (outer_shape[0], outer_shape[1], padded.shape[2]))
        return piece.reshape(-1, padded.shape[2])

    def cut_local(field, lat_index, lon_index):
        start = (lat_index * BAND_ROWS, lon_index * SECTOR_COLS, lat_index * 0)
        piece = lax.dynamic_slice(field, start, (BAND_ROWS, SECTOR_COLS, field.shape[2]))
        return piece.reshape(-1, field.shape[2])

    def first_pass(block):
        lat_index = block // N_LON
        lon_index = block % N_LON
        allowed = neighbour_mask(pole_reach, lat_index, lon_index, BAND_ROWS, SECTOR_COLS, ROWS, COLS)
        return query_block(cut_local(query_field, lat_index, lon_index), cut_outer(padded_key, lat_index, lon_index), cut_outer(padded_value, lat_index, lon_index), cut_local(out_grad, lat_index, lon_index), allowed)
    blocks = jnp.arange(N_LAT * N_LON, dtype=jnp.int32)
    log_stack, dot_stack, query_stack = lax.map(first_pass, blocks)
    padded_log = pad_global(to_grid(log_stack))
    padded_dot = pad_global(to_grid(dot_stack))

    def second_pass(block):
        lat_index = block // N_LON
        lon_index = block % N_LON
        allowed = neighbour_mask(pole_reach, lat_index, lon_index, BAND_ROWS, SECTOR_COLS, ROWS, COLS)
        return key_block(cut_local(key_field, lat_index, lon_index), cut_local(value_field, lat_index, lon_index), cut_outer(padded_query, lat_index, lon_index), cut_outer(padded_grad, lat_index, lon_index), cut_outer(padded_log, lat_index, lon_index), cut_outer(padded_dot, lat_index, lon_index), allowed)
    key_stack, value_stack = lax.map(second_pass, blocks)
    return (to_grid(query_stack), to_grid(key_stack), to_grid(value_stack))
```

```python
import functools
import math

import jax
import jax.numpy as jnp
from jax import lax
from jax.experimental import pallas as pl
from jax.experimental.pallas import tpu as pltpu
from jax.sharding import PartitionSpec as P

HEAD_DIM = 32
RADIUS = 6
STRIP = 8
LANES = 128
NEG = -1e30
LOG2E = 1.4426950408889634


def routes(lat_count, lon_count):
    half = lon_count // 2
    pair, around, across = [], [], []
    for i in range(lat_count):
        for j in range(lon_count):
            me = i * lon_count + j
            pair.append((me, (i ^ 1) * lon_count + j))
            step = 1 if i % 2 == 0 else -1
            around.append((me, i * lon_count + (j + step) % lon_count))
            other = i - 1 if i % 2 == 0 else i + 1
            if 0 <= other < lat_count:
                across.append((me, other * lon_count + j))
            else:
                across.append((me, i * lon_count + (j + half) % lon_count))
    return pair, around, across


def sizes(block_rows, block_cols):
    span = block_rows + RADIUS
    own = block_rows * block_cols
    oth = RADIUS * block_cols
    strip = span * STRIP
    off = RADIUS * (block_cols + 2 * STRIP)
    return own, oth, strip, strip, off


def mask_kernel(rows, cols, lat_count, lon_count, sc_ref, reach_ref, reach_t_ref, out_ref):
    lat, lon = sc_ref[0], sc_ref[1]
    total_rows, total_cols = rows * lat_count, cols * lon_count
    half = total_cols // 2
    odd = lax.rem(lat, 2)
    row0, col0 = lat * rows, lon * cols
    own, oth, strip, _, off = sizes(rows, cols)
    outer = own + 2 * strip + oth + off
    t = lax.broadcasted_iota(jnp.int32, (1, outer), 1)
    is_north, is_south = lat == 0, lat == lat_count - 1
    sender_odd = jnp.where(is_north | is_south, odd, 1 - odd)

    def split(index, width):
        shift = width.bit_length() - 1
        return lax.shift_right_logical(index, shift), index & (width - 1)

    r_own, c_own = split(t, cols)
    u = t - own
    r_oth, c_oth = split(u, cols)
    r_oth = r_oth + jnp.where(odd == 0, rows, -RADIUS)
    first = jnp.where(odd == 0, 0, -RADIUS)
    u = t - (own + oth)
    r_a, c_a = split(u, STRIP)
    r_a, c_a = r_a + first, c_a + jnp.where(odd == 0, -STRIP, cols)
    u = t - (own + oth + strip)
    r_b, c_b = split(u, STRIP)
    r_b, c_b = r_b + first, c_b + jnp.where(odd == 0, cols, -STRIP)
    u = t - (own + oth + 2 * strip)
    width = cols + 2 * STRIP
    r_off, x = split(u, width)
    r_off = jnp.where(
        is_north & (odd == 0),
        -1 - r_off,
        jnp.where(
            is_south & (odd == 1),
            rows + RADIUS - 1 - r_off,
            r_off + jnp.where(odd == 0, -RADIUS, rows),
        ),
    )
    first_at = jnp.where(sender_odd == 0, -STRIP, cols)
    second_at = jnp.where(sender_odd == 0, cols, -STRIP)
    c_off = jnp.where(
        x < cols, x, jnp.where(x < cols + STRIP, x - cols + first_at, x - cols - STRIP + second_at)
    )
    at = [own, own + oth, own + oth + strip, own + oth + 2 * strip]
    r_key = jnp.where(
        t < at[0],
        r_own,
        jnp.where(t < at[1], r_oth, jnp.where(t < at[2], r_a, jnp.where(t < at[3], r_b, r_off))),
    )
    c_key = jnp.where(
        t < at[0],
        c_own,
        jnp.where(t < at[1], c_oth, jnp.where(t < at[2], c_a, jnp.where(t < at[3], c_b, c_off))),
    )
    g_key = r_key + row0
    turned = lax.rem(c_key + (col0 + half + total_cols), total_cols)
    pick = lax.broadcasted_iota(jnp.int32, (total_cols, outer), 0) == turned
    north_key = jnp.sum(jnp.where(pick, reach_t_ref[:, 0:1], 0.0), axis=0, keepdims=True)
    south_key = jnp.sum(jnp.where(pick, reach_t_ref[:, 1:2], 0.0), axis=0, keepdims=True)
    g_f = g_key.astype(jnp.float32)
    behind_n = g_key < 0
    behind_s = g_key >= total_rows
    spare = jnp.where(
        behind_n, north_key + 1.0 + g_f, jnp.where(behind_s, south_key + total_rows - g_f, 1.0)
    )
    valid = jnp.where(spare > 0.5, 1.0, 0.0)
    n = lax.broadcasted_iota(jnp.int32, (own, 1), 0)
    r_n, c_n = split(n, cols)
    pick_n = lax.broadcasted_iota(jnp.int32, (own, total_cols), 1) == (c_n + col0)
    north_n = jnp.sum(jnp.where(pick_n, reach_ref[0:1, :], 0.0), axis=1, keepdims=True)
    south_n = jnp.sum(jnp.where(pick_n, reach_ref[1:2, :], 0.0), axis=1, keepdims=True)
    g_n = (r_n + row0).astype(jnp.float32)
    north_ok = jnp.where(north_n > g_n, 1.0, 0.0)
    south_ok = jnp.where(south_n > total_rows - 1 - g_n, 1.0, 0.0)
    need_n = jnp.where(behind_n, 1.0, 0.0)
    need_s = jnp.where(behind_s, 1.0, 0.0)
    near = (jnp.abs(r_key - r_n) <= RADIUS) & (jnp.abs(c_key - c_n) <= RADIUS)
    ok = jnp.where(near, 1.0, 0.0) * valid
    ok = jnp.where(need_n > north_ok, 0.0, ok)
    ok = jnp.where(need_s > south_ok, 0.0, ok)
    out_ref[...] = jnp.where(ok > 0.5, 0.0, NEG)


def assemble(target, own, oth, first, second, off, odd, rows, cols):
    n_own, n_oth, n_strip, _, n_off = sizes(rows, cols)
    at = 0
    target[0:n_own] = own
    at += n_own
    skip = rows - RADIUS
    start = pl.multiple_of(odd * (skip * cols), skip * cols)
    target[at : at + n_oth] = oth[pl.ds(start, n_oth)]
    at += n_oth
    start = pl.multiple_of(odd * (skip * STRIP), skip * STRIP)
    for piece in (first, second):
        target[at : at + n_strip] = piece[pl.ds(start, n_strip)]
        at += n_strip
    target[at : at + n_off] = off[...]


NT = (((1,), (1,)), ((), ()))


def query_kernel(
    rows, cols, sc_ref, q_ref, k_ref, v_ref, g_ref, oth_ref, lc_ref, s2_ref, off_ref, bias_ref,
    dq_ref, st_ref, kall, vall, stat,
):
    odd = lax.rem(sc_ref[0], 2)
    for i, (target, own) in enumerate(((kall, k_ref), (vall, v_ref))):
        assemble(
            target, own[...], oth_ref.at[i], lc_ref.at[i], s2_ref.at[i], off_ref.at[i], odd, rows, cols
        )
    own_count = rows * cols
    scale = 1.0 / math.sqrt(HEAD_DIM)
    lane = lax.broadcasted_iota(jnp.int32, (own_count, LANES), 1)
    per = LANES // HEAD_DIM
    heads = q_ref.shape[1] // HEAD_DIM
    stat[...] = jnp.zeros_like(stat)

    def group(g, carry):
        at = pl.ds(pl.multiple_of(g * LANES, LANES), LANES)
        kg, vg = kall[:, at], vall[:, at]
        qg, gg = q_ref[:, at], g_ref[:, at]
        total = jnp.zeros((own_count, LANES), jnp.float32)
        stats = stat[...]
        for j in range(per):
            mine = (lane >= j * HEAD_DIM) & (lane < (j + 1) * HEAD_DIM)
            qj = jnp.where(mine, qg, jnp.zeros_like(qg))
            gj = jnp.where(mine, gg, jnp.zeros_like(gg))
            s = lax.dot_general(qj, kg, NT, preferred_element_type=jnp.float32)
            gp = lax.dot_general(gj, vg, NT, preferred_element_type=jnp.float32)
            s = s * (scale * LOG2E) + bias_ref[...]
            top = jnp.max(s, axis=1, keepdims=True)
            e = jnp.exp2(s - top)
            total_e = jnp.sum(e, axis=1, keepdims=True)
            p = e * (1.0 / total_e)
            ph = p.astype(jnp.bfloat16).astype(jnp.float32)
            dot = jnp.sum(ph * gp, axis=1, keepdims=True)
            ds = (p * (gp - dot)).astype(jnp.bfloat16)
            dq = jnp.dot(ds, kg, preferred_element_type=jnp.float32)
            total = jnp.where(mine, dq, total)
            h = g * per + j
            log_total = top + jnp.log2(total_e)
            stats = jnp.where((lane == h) | (lane == h + heads) | (lane == h + 2 * heads), log_total, stats)
            base = h + 3 * heads
            stats = jnp.where(
                (lane == base) | (lane == base + heads) | (lane == base + 2 * heads), dot, stats
            )
        stat[...] = stats
        dq_ref[:, at] = (total * scale).astype(jnp.bfloat16)
        return carry

    lax.fori_loop(0, q_ref.shape[1] // LANES, group, 0)
    x = stat[...]
    high = x.astype(jnp.bfloat16).astype(jnp.float32)
    rest = x - high
    mid = rest.astype(jnp.bfloat16).astype(jnp.float32)
    low = rest - mid
    third = lax.rem(lax.shift_right_logical(lane, heads.bit_length() - 1), 3)
    st_ref[...] = jnp.where(third == 0, high, jnp.where(third == 1, mid, low)).astype(jnp.bfloat16)


def key_kernel(
    rows, cols, sc_ref, q_ref, k_ref, v_ref, g_ref, oth_ref, lc_ref, s2_ref, off_ref,
    st_ref, st_oth_ref, st_lc_ref, st_s2_ref, st_off_ref, bias_ref,
    dk_ref, dv_ref, qall, gall, stall, stat_rows,
):
    odd = lax.rem(sc_ref[0], 2)
    for i, (target, own) in enumerate(((qall, q_ref), (gall, g_ref))):
        assemble(
            target, own[...], oth_ref.at[i], lc_ref.at[i], s2_ref.at[i], off_ref.at[i], odd, rows, cols
        )
    assemble(stall, st_ref[...], st_oth_ref, st_lc_ref, st_s2_ref, st_off_ref, odd, rows, cols)
    own_count = rows * cols
    scale = 1.0 / math.sqrt(HEAD_DIM)
    lane = lax.broadcasted_iota(jnp.int32, (own_count, LANES), 1)
    per = LANES // HEAD_DIM
    heads = q_ref.shape[1] // HEAD_DIM
    row = lax.broadcasted_iota(jnp.int32, (2 * heads, LANES), 0)
    col = lax.broadcasted_iota(jnp.int32, (2 * heads, LANES), 1)
    start = jnp.where(row < heads, row, row + 2 * heads)
    choose = (col == start) | (col == start + heads) | (col == start + 2 * heads)
    choose = jnp.where(choose, 1.0, 0.0).astype(jnp.bfloat16)
    stat_rows[...] = lax.dot_general(choose, stall[...], NT, preferred_element_type=jnp.float32)

    def group(g, carry):
        at = pl.ds(pl.multiple_of(g * LANES, LANES), LANES)
        qg, gg = qall[:, at], gall[:, at]
        kg, vg = k_ref[:, at], v_ref[:, at]
        dk_total = jnp.zeros((own_count, LANES), jnp.float32)
        dv_total = jnp.zeros((own_count, LANES), jnp.float32)
        for j in range(per):
            mine = (lane >= j * HEAD_DIM) & (lane < (j + 1) * HEAD_DIM)
            kj = jnp.where(mine, kg, jnp.zeros_like(kg))
            vj = jnp.where(mine, vg, jnp.zeros_like(vg))
            s = lax.dot_general(kj, qg, NT, preferred_element_type=jnp.float32)
            gp = lax.dot_general(vj, gg, NT, preferred_element_type=jnp.float32)
            h = g * per + j
            log_total = stat_rows[pl.ds(h, 1), :]
            dot = stat_rows[pl.ds(h + heads, 1), :]
            p = jnp.exp2(s * (scale * LOG2E) + (bias_ref[...] - log_total))
            ph = p.astype(jnp.bfloat16)
            dv = jnp.dot(ph, gg, preferred_element_type=jnp.float32)
            ds = (p * (gp - dot)).astype(jnp.bfloat16)
            dk = jnp.dot(ds, qg, preferred_element_type=jnp.float32)
            dk_total = jnp.where(mine, dk, dk_total)
            dv_total = jnp.where(mine, dv, dv_total)
        dk_ref[:, at] = (dk_total * scale).astype(jnp.bfloat16)
        dv_ref[:, at] = dv_total.astype(jnp.bfloat16)
        return carry

    lax.fori_loop(0, q_ref.shape[1] // LANES, group, 0)


def shards(lat_count, lon_count, query, key, value, grad, pole_reach):
    rows, cols, width = query.shape
    lat, lon = lax.axis_index("lat"), lax.axis_index("lon")
    odd = lax.rem(lat, 2)
    even = odd == 0
    pair, around, across = routes(lat_count, lon_count)
    axes = ("lat", "lon")
    n_own, n_oth, n_strip, _, n_off = sizes(rows, cols)
    outer = n_own + n_oth + 2 * n_strip + n_off
    place = jnp.stack([lat, lon]).astype(jnp.int32)

    smem = pl.BlockSpec(memory_space=pltpu.SMEM)
    vmem = pl.BlockSpec(memory_space=pltpu.VMEM)

    def call(body, out_shape, n_in, scratch, flops):
        return pl.pallas_call(
            body,
            out_shape=out_shape,
            in_specs=[smem] + [vmem] * (n_in - 1),
            out_specs=jax.tree.map(lambda _: vmem, out_shape),
            scratch_shapes=scratch,
            compiler_params=pltpu.CompilerParams(vmem_limit_bytes=48 << 20),
            cost_estimate=pl.CostEstimate(flops=flops, bytes_accessed=4 << 20, transcendentals=0),
        )

    reach = pole_reach.astype(jnp.float32)
    bias = call(
        functools.partial(mask_kernel, rows, cols, lat_count, lon_count),
        jax.ShapeDtypeStruct((n_own, outer), jnp.float32), 3, [], 1 << 20,
    )(place, reach, reach.T)

    def strip_of(mine, other):
        axis = mine.ndim - 3
        at = jnp.where(even, cols - STRIP, 0)
        mine = lax.dynamic_slice_in_dim(mine, at, STRIP, axis + 1)
        other = lax.dynamic_slice_in_dim(other, at, STRIP, axis + 1)
        top, low = jnp.where(even, mine, other), jnp.where(even, other, mine)
        both = jnp.concatenate([top, low], axis=axis)
        return both.reshape(both.shape[:axis] + (2 * rows * STRIP, both.shape[-1]))

    def edge_of(mine, first, second):
        axis = mine.ndim - 3
        lead = mine.shape[:axis]
        tail = mine.shape[-1:]
        parts = [lax.dynamic_slice_in_dim(mine, jnp.where(even, 0, rows - RADIUS), RADIUS, axis)]
        for piece in (first, second):
            piece = piece.reshape(lead + (2 * rows, STRIP) + tail)
            parts.append(
                lax.dynamic_slice_in_dim(piece, jnp.where(even, 0, 2 * rows - RADIUS), RADIUS, axis)
            )
        return jnp.concatenate(parts, axis=axis + 1).reshape(lead + (n_off,) + tail)

    def send(block, route):
        return lax.ppermute(block, axes, route)

    def halo(mine, other):
        first = send(strip_of(mine, other), around)
        second = send(first, pair)
        off = send(edge_of(mine, first, second), across)
        return first, second, off

    def flat(field):
        return field.reshape(field.shape[:-3] + (n_own, field.shape[-1]))

    mine = jnp.stack([key, value, query, grad])
    other = send(mine, pair)
    kv = halo(mine[:2], other[:2])
    qg = halo(mine[2:], other[2:])
    fields = tuple(flat(x) for x in (query, key, value, grad))
    vm = lambda shape, dtype=jnp.bfloat16: pltpu.VMEM(shape, dtype)
    local = jax.ShapeDtypeStruct((n_own, width), jnp.bfloat16)
    d_query, stats = call(
        functools.partial(query_kernel, rows, cols),
        (local, jax.ShapeDtypeStruct((n_own, LANES), jnp.bfloat16)),
        10,
        [vm((outer, width)), vm((outer, width)), vm((n_own, LANES), jnp.float32)],
        1 << 29,
    )(place, *fields, flat(other[:2]), *kv, bias)
    stats_grid = stats.reshape(rows, cols, LANES)
    stats_other = send(stats_grid, pair)
    st = halo(stats_grid, stats_other)
    d_key, d_value = call(
        functools.partial(key_kernel, rows, cols),
        (local, local),
        15,
        [
            vm((outer, width)), vm((outer, width)), vm((outer, LANES)),
            vm((2 * (width // HEAD_DIM), outer), jnp.float32),
        ],
        1 << 29,
    )(place, *fields, flat(other[2:]), *qg, stats, flat(stats_other), *st, bias)
    shape = (rows, cols, width)
    return d_query.reshape(shape), d_key.reshape(shape), d_value.reshape(shape)


def solution(mesh):
    field = P("lat", "lon", None)
    return jax.shard_map(
        functools.partial(shards, mesh.shape["lat"], mesh.shape["lon"]),
        mesh=mesh,
        in_specs=(field, field, field, field, P()),
        out_specs=(field, field, field),
        check_vma=False,
    )
```

```python
import functools
import math

import jax
import jax.numpy as jnp
from jax import lax
from jax.experimental import pallas as pl
from jax.experimental.pallas import tpu as pltpu
from jax.sharding import PartitionSpec as P

HEAD_DIM = 32
RADIUS = 6
STRIP = 8
LANES = 128
NEG = -1e30
LOG2E = 1.4426950408889634


def routes(lat_count, lon_count):
    half = lon_count // 2
    pair, around, across = [], [], []
    for i in range(lat_count):
        for j in range(lon_count):
            me = i * lon_count + j
            pair.append((me, (i ^ 1) * lon_count + j))
            step = 1 if i % 2 == 0 else -1
            around.append((me, i * lon_count + (j + step) % lon_count))
            other = i - 1 if i % 2 == 0 else i + 1
            if 0 <= other < lat_count:
                across.append((me, other * lon_count + j))
            else:
                across.append((me, i * lon_count + (j + half) % lon_count))
    return pair, around, across


def sizes(rows, cols):
    own, strip, off = rows * cols, 2 * rows * STRIP, RADIUS * (cols + 2 * STRIP)
    return own, own, strip, strip, off


def mask_kernel(rows, cols, lat_count, lon_count, sc_ref, reach_ref, reach_t_ref, out_ref, out_t_ref):
    lat, lon = sc_ref[0], sc_ref[1]
    total_rows, total_cols = rows * lat_count, cols * lon_count
    half = total_cols // 2
    odd = lax.rem(lat, 2)
    row0, col0 = lat * rows, lon * cols
    own, oth, strip, _, off = sizes(rows, cols)
    outer = own + 2 * strip + oth + off
    t = lax.broadcasted_iota(jnp.int32, (1, outer), 1)
    is_north, is_south = lat == 0, lat == lat_count - 1
    sender_odd = jnp.where(is_north | is_south, odd, 1 - odd)

    def split(index, width):
        shift = width.bit_length() - 1
        return lax.shift_right_logical(index, shift), index & (width - 1)

    r_own, c_own = split(t, cols)
    u = t - own
    r_oth, c_oth = split(u, cols)
    r_oth = r_oth + jnp.where(odd == 0, rows, -rows)
    first = jnp.where(odd == 0, 0, -rows)
    u = t - (own + oth)
    r_a, c_a = split(u, STRIP)
    r_a, c_a = r_a + first, c_a + jnp.where(odd == 0, -STRIP, cols)
    u = t - (own + oth + strip)
    r_b, c_b = split(u, STRIP)
    r_b, c_b = r_b + first, c_b + jnp.where(odd == 0, cols, -STRIP)
    u = t - (own + oth + 2 * strip)
    width = cols + 2 * STRIP
    r_off, x = split(u, width)
    r_off = jnp.where(
        is_north & (odd == 0),
        -1 - r_off,
        jnp.where(
            is_south & (odd == 1),
            rows + RADIUS - 1 - r_off,
            r_off + jnp.where(odd == 0, -RADIUS, rows),
        ),
    )
    first_at = jnp.where(sender_odd == 0, -STRIP, cols)
    second_at = jnp.where(sender_odd == 0, cols, -STRIP)
    c_off = jnp.where(
        x < cols, x, jnp.where(x < cols + STRIP, x - cols + first_at, x - cols - STRIP + second_at)
    )
    at = [own, own + oth, own + oth + strip, own + oth + 2 * strip]
    r_key = jnp.where(
        t < at[0],
        r_own,
        jnp.where(t < at[1], r_oth, jnp.where(t < at[2], r_a, jnp.where(t < at[3], r_b, r_off))),
    )
    c_key = jnp.where(
        t < at[0],
        c_own,
        jnp.where(t < at[1], c_oth, jnp.where(t < at[2], c_a, jnp.where(t < at[3], c_b, c_off))),
    )
    g_key = r_key + row0
    turned = lax.rem(c_key + (col0 + half + total_cols), total_cols)
    pick = lax.broadcasted_iota(jnp.int32, (total_cols, outer), 0) == turned
    north_key = jnp.sum(jnp.where(pick, reach_t_ref[:, 0:1], 0.0), axis=0, keepdims=True)
    south_key = jnp.sum(jnp.where(pick, reach_t_ref[:, 1:2], 0.0), axis=0, keepdims=True)
    g_f = g_key.astype(jnp.float32)
    behind_n = g_key < 0
    behind_s = g_key >= total_rows
    spare = jnp.where(
        behind_n, north_key + 1.0 + g_f, jnp.where(behind_s, south_key + total_rows - g_f, 1.0)
    )
    valid = jnp.where(spare > 0.5, 1.0, 0.0)
    n = lax.broadcasted_iota(jnp.int32, (own, 1), 0)
    r_n, c_n = split(n, cols)
    pick_n = lax.broadcasted_iota(jnp.int32, (own, total_cols), 1) == (c_n + col0)
    north_n = jnp.sum(jnp.where(pick_n, reach_ref[0:1, :], 0.0), axis=1, keepdims=True)
    south_n = jnp.sum(jnp.where(pick_n, reach_ref[1:2, :], 0.0), axis=1, keepdims=True)
    g_n = (r_n + row0).astype(jnp.float32)
    north_ok = jnp.where(north_n > g_n, 1.0, 0.0)
    south_ok = jnp.where(south_n > total_rows - 1 - g_n, 1.0, 0.0)
    need_n = jnp.where(behind_n, 1.0, 0.0)
    need_s = jnp.where(behind_s, 1.0, 0.0)
    near = (jnp.abs(r_key - r_n) <= RADIUS) & (jnp.abs(c_key - c_n) <= RADIUS)
    ok = jnp.where(near, 1.0, 0.0) * valid
    ok = jnp.where(need_n > north_ok, 0.0, ok)
    ok = jnp.where(need_s > south_ok, 0.0, ok)
    bias = jnp.where(ok > 0.5, 0.0, NEG)
    out_ref[...] = bias
    out_t_ref[...] = bias.T


def assemble(target, *pieces):
    at = 0
    for piece in pieces:
        target[at : at + piece.shape[0]] = piece[...]
        at += piece.shape[0]


NT = (((1,), (1,)), ((), ()))
SCALE = 1.0 / math.sqrt(HEAD_DIM)


def lanes_of(shape, j):
    lane = lax.broadcasted_iota(jnp.int32, shape, 1)
    return (lane >= j * HEAD_DIM) & (lane < (j + 1) * HEAD_DIM)


def spread(x):
    per = LANES // HEAD_DIM
    return jnp.concatenate(
        [jnp.where(lanes_of(x.shape, j), x, jnp.zeros_like(x)) for j in range(per)], axis=0
    )


def gather(x):
    per = LANES // HEAD_DIM
    count = x.shape[0] // per
    total = x[0:count]
    for j in range(1, per):
        total = jnp.where(lanes_of((count, LANES), j), x[j * count : (j + 1) * count], total)
    return total


def part(x, j, axis):
    count = x.shape[axis] // (LANES // HEAD_DIM)
    return lax.slice_in_dim(x, j * count, (j + 1) * count, axis=axis)


def groups(width):
    for g in range(width // LANES):
        yield slice(g * LANES, (g + 1) * LANES), g * (LANES // HEAD_DIM)


def dot_nt(a, b):
    return lax.dot_general(a, b, NT, preferred_element_type=jnp.float32)


def partial_stats(q_ref, g_ref, keys, values, bias, top_ref, sum_ref, dot_ref):
    for at, first in groups(q_ref.shape[1]):
        s_all = dot_nt(keys[:, at], spread(q_ref[:, at]))
        gp_all = dot_nt(values[:, at], spread(g_ref[:, at]))
        for j in range(LANES // HEAD_DIM):
            s, gp = part(s_all, j, 1) * (SCALE * LOG2E) + bias, part(gp_all, j, 1)
            top = jnp.max(s, axis=0, keepdims=True)
            e = jnp.exp2(s - top)
            h = first + j
            top_ref[h : h + 1, :] = top
            sum_ref[h : h + 1, :] = jnp.sum(e, axis=0, keepdims=True)
            dot_ref[h : h + 1, :] = jnp.sum(e * gp, axis=0, keepdims=True)


def near_stats_kernel(
    q_ref, g_ref, k_ref, v_ref, k_oth, v_oth, lc_ref, s2_ref, bias_ref,
    kall_ref, vall_ref, top_ref, sum_ref, dot_ref,
):
    assemble(kall_ref, k_ref, k_oth, lc_ref.at[0], s2_ref.at[0])
    assemble(vall_ref, v_ref, v_oth, lc_ref.at[1], s2_ref.at[1])
    near = kall_ref.shape[0]
    partial_stats(
        q_ref, g_ref, kall_ref, vall_ref, bias_ref[0:near, :], top_ref, sum_ref, dot_ref
    )


def far_stats_kernel(
    q_ref, g_ref, off_ref, bias_ref, top_ref, sum_ref, dot_ref, st_ref, top2, sum2, dot2
):
    near = bias_ref.shape[0] - off_ref.shape[1]
    partial_stats(
        q_ref, g_ref, off_ref.at[0], off_ref.at[1], bias_ref[near:, :], top2, sum2, dot2
    )
    top = jnp.maximum(top_ref[...], top2[...])
    a, b = jnp.exp2(top_ref[...] - top), jnp.exp2(top2[...] - top)
    total = sum_ref[...] * a + sum2[...] * b
    log_total = top + jnp.log2(total)
    dot = (dot_ref[...] * a + dot2[...] * b) / total
    terms = []
    for x in (log_total, dot):
        high = x.astype(jnp.bfloat16).astype(jnp.float32)
        mid = (x - high).astype(jnp.bfloat16).astype(jnp.float32)
        terms += [high, mid, x - high - mid]
    count = sum(x.shape[0] for x in terms)
    terms.append(jnp.zeros((LANES - count, top.shape[1]), jnp.float32))
    st_ref[...] = jnp.concatenate(terms, axis=0).T.astype(jnp.bfloat16)


def query_kernel(q_ref, g_ref, kall_ref, vall_ref, off_ref, bias_ref, st_ref, dq_ref):
    heads = q_ref.shape[1] // HEAD_DIM
    near = kall_ref.shape[0]
    row = lax.broadcasted_iota(jnp.int32, (LANES, LANES), 0)

    def stat_of(h):
        choose = (row == h) | (row == h + heads) | (row == h + 2 * heads)
        choose = jnp.where(choose, 1.0, 0.0).astype(jnp.bfloat16)
        return jnp.dot(st_ref[...], choose, preferred_element_type=jnp.float32)

    def wide(x, count):
        return jnp.concatenate([x] * -(-count // LANES), axis=1)[:, :count]

    per = LANES // HEAD_DIM
    for at, first in groups(q_ref.shape[1]):
        sides = (
            (kall_ref[:, at], vall_ref[:, at], bias_ref[:, 0:near]),
            (off_ref[0, :, at], off_ref[1, :, at], bias_ref[:, near:]),
        )
        qs, gs = spread(q_ref[:, at]), spread(g_ref[:, at])
        logs = [stat_of(first + j) for j in range(per)]
        dots = [stat_of(first + j + 3 * heads) for j in range(per)]
        total = jnp.zeros((q_ref.shape[0], LANES), jnp.float32)
        for kg, vg, bias in sides:
            count = kg.shape[0]
            s, gp = dot_nt(qs, kg), dot_nt(gs, vg)
            ds = []
            for j in range(per):
                p = jnp.exp2(part(s, j, 0) * (SCALE * LOG2E) + (bias - wide(logs[j], count)))
                ds.append((p * (part(gp, j, 0) - wide(dots[j], count))).astype(jnp.bfloat16))
            ds = jnp.concatenate(ds, axis=0)
            total += gather(jnp.dot(ds, kg, preferred_element_type=jnp.float32))
        dq_ref[:, at] = (total * SCALE).astype(jnp.bfloat16)


def key_sums(k_ref, v_ref, queries, grads, stats, bias, stat_rows, finish):
    heads = k_ref.shape[1] // HEAD_DIM
    row = lax.broadcasted_iota(jnp.int32, (2 * heads, LANES), 0)
    col = lax.broadcasted_iota(jnp.int32, (2 * heads, LANES), 1)
    base = jnp.where(row < heads, row, row + 2 * heads)
    choose = (col == base) | (col == base + heads) | (col == base + 2 * heads)
    choose = jnp.where(choose, 1.0, 0.0).astype(jnp.bfloat16)
    stat_rows[...] = dot_nt(choose, stats[...])
    for at, first in groups(k_ref.shape[1]):
        qg, gg = queries[:, at], grads[:, at]
        s, gp = dot_nt(spread(k_ref[:, at]), qg), dot_nt(spread(v_ref[:, at]), gg)
        p_half, ds = [], []
        for j in range(LANES // HEAD_DIM):
            h = first + j
            log_total, dot = stat_rows[h : h + 1, :], stat_rows[h + heads : h + heads + 1, :]
            p = jnp.exp2(part(s, j, 0) * (SCALE * LOG2E) + (bias - log_total))
            p_half.append(p.astype(jnp.bfloat16))
            ds.append((p * (part(gp, j, 0) - dot)).astype(jnp.bfloat16))
        dv = jnp.dot(jnp.concatenate(p_half, axis=0), gg, preferred_element_type=jnp.float32)
        dk = jnp.dot(jnp.concatenate(ds, axis=0), qg, preferred_element_type=jnp.float32)
        finish(at, gather(dk), gather(dv))


def near_key_kernel(
    k_ref, v_ref, q_ref, g_ref, q_oth, g_oth, lc_ref, s2_ref,
    st_ref, st_oth, st_lc, st_s2, bias_ref, dk_ref, dv_ref, qall, gall, stall, stat_rows,
):
    assemble(qall, q_ref, q_oth, lc_ref.at[0], s2_ref.at[0])
    assemble(gall, g_ref, g_oth, lc_ref.at[1], s2_ref.at[1])
    assemble(stall, st_ref, st_oth, st_lc, st_s2)
    near = qall.shape[0]

    def finish(at, dk, dv):
        dk_ref[:, at], dv_ref[:, at] = dk, dv

    key_sums(k_ref, v_ref, qall, gall, stall, bias_ref[:, 0:near], stat_rows, finish)


def far_key_kernel(
    k_ref, v_ref, off_ref, st_off, bias_ref, dk_in, dv_in, dk_ref, dv_ref, stat_rows
):
    near = bias_ref.shape[1] - off_ref.shape[1]

    def finish(at, dk, dv):
        dk_ref[:, at] = ((dk_in[:, at] + dk) * SCALE).astype(jnp.bfloat16)
        dv_ref[:, at] = (dv_in[:, at] + dv).astype(jnp.bfloat16)

    key_sums(
        k_ref, v_ref, off_ref.at[0], off_ref.at[1], st_off, bias_ref[:, near:], stat_rows, finish
    )


def shards(lat_count, lon_count, query, key, value, grad, pole_reach):
    rows, cols, width = query.shape
    lat, lon = lax.axis_index("lat"), lax.axis_index("lon")
    odd = lax.rem(lat, 2)
    even = odd == 0
    pair, around, across = routes(lat_count, lon_count)
    axes = ("lat", "lon")
    n_own, n_oth, n_strip, _, n_off = sizes(rows, cols)
    near = n_own + n_oth + 2 * n_strip
    outer = near + n_off
    place = jnp.stack([lat, lon]).astype(jnp.int32)

    smem = pl.BlockSpec(memory_space=pltpu.SMEM)
    vmem = pl.BlockSpec(memory_space=pltpu.VMEM)

    def call(body, outs, operands, scratch=(), flops=1 << 28, scalars=False):
        return pl.pallas_call(
            body,
            out_shape=outs,
            in_specs=[smem] * scalars + [vmem] * (len(operands) - scalars),
            out_specs=jax.tree.map(lambda _: vmem, outs),
            scratch_shapes=scratch,
            compiler_params=pltpu.CompilerParams(vmem_limit_bytes=32 << 20),
            cost_estimate=pl.CostEstimate(flops=flops, bytes_accessed=4 << 20, transcendentals=0),
        )(*operands)

    def array(*shape, dtype=jnp.bfloat16):
        return jax.ShapeDtypeStruct(shape, dtype)

    f32 = jnp.float32
    heads = width // HEAD_DIM
    reach = pole_reach.astype(f32)
    bias, bias_t = call(
        functools.partial(mask_kernel, rows, cols, lat_count, lon_count),
        (array(n_own, outer, dtype=f32), array(outer, n_own, dtype=f32)),
        (place, reach, reach.T),
        scalars=True,
    )

    def strip_of(mine, other):
        at = jnp.where(even, cols - STRIP, 0)
        mine = lax.dynamic_slice_in_dim(mine, at, STRIP, 1)
        other = lax.dynamic_slice_in_dim(other, at, STRIP, 1)
        top, low = jnp.where(even, mine, other), jnp.where(even, other, mine)
        return jnp.concatenate([top, low], axis=0).reshape(2 * rows * STRIP, -1)

    def edge_of(mine, first, second):
        parts = [lax.dynamic_slice_in_dim(mine, jnp.where(even, 0, rows - RADIUS), RADIUS, 0)]
        for piece in (first, second):
            piece = piece.reshape(2 * rows, STRIP, -1)
            parts.append(
                lax.dynamic_slice_in_dim(piece, jnp.where(even, 0, 2 * rows - RADIUS), RADIUS, 0)
            )
        return jnp.concatenate(parts, axis=1).reshape(n_off, -1)

    def send(block, route):
        return lax.ppermute(block, axes, route)

    def stacked(parts):
        return jnp.stack(parts) if len(parts) > 1 else parts[0]

    def strips(mine, other):
        return stacked([strip_of(a, b) for a, b in zip(mine, other)])

    def edges(mine, first, second):
        if len(mine) == 1:
            return edge_of(mine[0], first, second)
        return jnp.stack([edge_of(a, first[i], second[i]) for i, a in enumerate(mine)])

    def flat(field):
        return field.reshape(n_own, field.shape[-1])

    key_o, value_o = send(key, pair), send(value, pair)
    kv, kv_o = (key, value), (key_o, value_o)
    kv_1 = send(strips(kv, kv_o), around)
    kv_2 = send(kv_1, pair)
    kv_off = send(edges(kv, kv_1, kv_2), across)

    query_s, grad_s, _ = lax.optimization_barrier((query, grad, key_o))
    query_o, grad_o = send(query_s, pair), send(grad_s, pair)
    qg, qg_o = (query, grad), (query_o, grad_o)
    qg_1 = send(strips(qg, qg_o), around)

    q, k, v, g = (flat(x) for x in (query, key, value, grad))
    stat = array(heads, n_own, dtype=f32)
    kall, vall, *near_stats = call(
        near_stats_kernel,
        (array(near, width), array(near, width), stat, stat, stat),
        (q, g, k, v, flat(key_o), flat(value_o), kv_1, kv_2, bias_t),
    )
    stats = call(
        far_stats_kernel,
        array(n_own, LANES),
        (q, g, kv_off, bias_t, *near_stats),
        [pltpu.VMEM((heads, n_own), f32)] * 3,
    )
    stats_grid = stats.reshape(rows, cols, LANES)
    stats_o = send(stats_grid, pair)
    st_1 = send(strip_of(stats_grid, stats_o), around)
    d_query = call(query_kernel, array(n_own, width), (q, g, kall, vall, kv_off, bias, stats))
    st_1, d_query = lax.optimization_barrier((st_1, d_query))
    st_2 = send(st_1, pair)
    st_off = send(edge_of(stats_grid, st_1, st_2), across)

    qg_1, _ = lax.optimization_barrier((qg_1, stats_o))
    qg_2 = send(qg_1, pair)
    qg_off = send(edges(qg, qg_1, qg_2), across)

    sums = array(n_own, width, dtype=f32)
    d_key, d_value = call(
        near_key_kernel,
        (sums, sums),
        (
            k, v, q, g, flat(query_o), flat(grad_o), qg_1, qg_2,
            stats, flat(stats_o), st_1, st_2, bias,
        ),
        [
            pltpu.VMEM((near, width), jnp.bfloat16),
            pltpu.VMEM((near, width), jnp.bfloat16),
            pltpu.VMEM((near, LANES), jnp.bfloat16),
            pltpu.VMEM((2 * heads, near), f32),
        ],
    )
    d_key, d_value = call(
        far_key_kernel,
        (array(n_own, width), array(n_own, width)),
        (k, v, qg_off, st_off, bias, d_key, d_value),
        [pltpu.VMEM((2 * heads, n_off), f32)],
    )
    shape = (rows, cols, width)
    return d_query.reshape(shape), d_key.reshape(shape), d_value.reshape(shape)


def solution(mesh):
    field = P("lat", "lon", None)
    return jax.shard_map(
        functools.partial(shards, mesh.shape["lat"], mesh.shape["lon"]),
        mesh=mesh,
        in_specs=(field, field, field, field, P()),
        out_specs=(field, field, field),
        check_vma=False,
    )
```

```python
import functools
import math

import jax
import jax.numpy as jnp
import numpy as np
from jax import lax
from jax.experimental import pallas as pl
from jax.experimental.pallas import tpu as pltpu
from jax.sharding import PartitionSpec as P

HEAD_DIM = 32
RADIUS = 6
LANES = 128
NEG = -1e30
LOG2E = 1.4426950408889634


def routes(lat_count, lon_count):
    half = lon_count // 2
    pair, around, across = [], [], []
    for i in range(lat_count):
        for j in range(lon_count):
            me = i * lon_count + j
            pair.append((me, (i ^ 1) * lon_count + j))
            step = 1 if i % 2 == 0 else -1
            around.append((me, i * lon_count + (j + step) % lon_count))
            other = i - 1 if i % 2 == 0 else i + 1
            if 0 <= other < lat_count:
                across.append((me, other * lon_count + j))
            else:
                across.append((me, i * lon_count + (j + half) % lon_count))
    return pair, around, across


def pieces(rows, cols):
    corners = 2 * RADIUS * RADIUS
    pad = -corners % 16
    strip = 2 * rows * RADIUS
    return rows * cols, rows * cols, strip, strip, RADIUS * cols, corners + pad


def layout(rows, cols, odd, pole):
    west, east = range(-RADIUS, 0), range(cols, cols + RADIUS)
    mine, other = range(0, rows), range(-rows, 0) if odd else range(rows, 2 * rows)
    beyond = range(rows, rows + RADIUS) if odd else range(-RADIUS, 0)
    if pole:
        beyond = beyond[::-1]
    sender_odd = odd if pole else not odd
    places = [(r, c) for r in range(rows) for c in range(cols)]
    places += [(r + (-rows if odd else rows), c) for r, c in places]
    first, second = (east, west) if odd else (west, east)
    for side, bands in ((first, (mine, other)), (second, (other, mine))):
        places += [(r, c) for band in bands for r in band for c in side]
    places += [(r, c) for r in beyond for c in range(cols)]
    for side in (east, west) if sender_odd else (west, east):
        places += [(r, c) for r in beyond for c in side]
    nowhere = (1 << 20, 0)
    places += [nowhere] * (sum(pieces(rows, cols)) - len(places))
    return np.array(places, np.int32).T


def mask_kernel(
    rows, cols, lat_count, lon_count, sc_ref, reach_ref, reach_t_ref, table_ref,
    near_ref, far_ref, out_t_ref,
):
    lat, lon = sc_ref[0], sc_ref[1]
    total_rows, total_cols = rows * lat_count, cols * lon_count
    odd = lax.rem(lat, 2)
    pole = jnp.where(jnp.where(odd == 0, lat, lat_count - 1 - lat) == 0, 1, 0)
    row0, col0 = lat * rows, lon * cols
    which = 2 * (2 * odd + pole)
    r_key = table_ref[pl.ds(which, 1), :]
    c_key = table_ref[pl.ds(which + 1, 1), :]
    outer = r_key.shape[1]
    g_key = r_key + row0
    turned = lax.rem(c_key + (col0 + total_cols // 2 + total_cols), total_cols)
    pick = lax.broadcasted_iota(jnp.int32, (total_cols, outer), 0) == turned
    north_key = jnp.sum(jnp.where(pick, reach_t_ref[:, 0:1], 0.0), axis=0, keepdims=True)
    south_key = jnp.sum(jnp.where(pick, reach_t_ref[:, 1:2], 0.0), axis=0, keepdims=True)
    g_f = g_key.astype(jnp.float32)
    behind_n = g_key < 0
    behind_s = g_key >= total_rows
    spare = jnp.where(
        behind_n, north_key + 1.0 + g_f, jnp.where(behind_s, south_key + total_rows - g_f, 1.0)
    )
    valid = jnp.where(spare > 0.5, 1.0, 0.0)
    n = lax.broadcasted_iota(jnp.int32, (rows * cols, 1), 0)
    shift = cols.bit_length() - 1
    r_n, c_n = lax.shift_right_logical(n, shift), n & (cols - 1)
    pick_n = lax.broadcasted_iota(jnp.int32, (rows * cols, total_cols), 1) == (c_n + col0)
    north_n = jnp.sum(jnp.where(pick_n, reach_ref[0:1, :], 0.0), axis=1, keepdims=True)
    south_n = jnp.sum(jnp.where(pick_n, reach_ref[1:2, :], 0.0), axis=1, keepdims=True)
    g_n = (r_n + row0).astype(jnp.float32)
    north_ok = jnp.where(north_n > g_n, 1.0, 0.0)
    south_ok = jnp.where(south_n > total_rows - 1 - g_n, 1.0, 0.0)
    need_n = jnp.where(behind_n, 1.0, 0.0)
    need_s = jnp.where(behind_s, 1.0, 0.0)
    near = (jnp.abs(r_key - r_n) <= RADIUS) & (jnp.abs(c_key - c_n) <= RADIUS)
    ok = jnp.where(near, 1.0, 0.0) * valid
    ok = jnp.where(need_n > north_ok, 0.0, ok)
    ok = jnp.where(need_s > south_ok, 0.0, ok)
    bias = jnp.where(ok > 0.5, 0.0, NEG)
    count = near_ref.shape[1]
    near_ref[...] = bias[:, 0:count]
    far_ref[...] = bias[:, count:]
    out_t_ref[...] = bias.T


def assemble(target, *pieces):
    at = 0
    for piece in pieces:
        target[at : at + piece.shape[0]] = piece[...]
        at += piece.shape[0]


NT = (((1,), (1,)), ((), ()))
SCALE = 1.0 / math.sqrt(HEAD_DIM)


def lanes_of(shape, j):
    lane = lax.broadcasted_iota(jnp.int32, shape, 1)
    return (lane >= j * HEAD_DIM) & (lane < (j + 1) * HEAD_DIM)


def spread(x):
    per = LANES // HEAD_DIM
    return jnp.concatenate(
        [jnp.where(lanes_of(x.shape, j), x, jnp.zeros_like(x)) for j in range(per)], axis=0
    )


def gather(x):
    per = LANES // HEAD_DIM
    count = x.shape[0] // per
    total = x[0:count]
    for j in range(1, per):
        total = jnp.where(lanes_of((count, LANES), j), x[j * count : (j + 1) * count], total)
    return total


def part(x, j, axis):
    count = x.shape[axis] // (LANES // HEAD_DIM)
    return lax.slice_in_dim(x, j * count, (j + 1) * count, axis=axis)


def groups(width):
    for g in range(width // LANES):
        yield slice(g * LANES, (g + 1) * LANES), g * (LANES // HEAD_DIM)


def dot_nt(a, b):
    return lax.dot_general(a, b, NT, preferred_element_type=jnp.float32)


def partial_stats(q_ref, g_ref, keys, values, bias, top_ref, sum_ref, dot_ref):
    for at, first in groups(q_ref.shape[1]):
        s_all = dot_nt(keys[:, at], spread(q_ref[:, at]))
        gp_all = dot_nt(values[:, at], spread(g_ref[:, at]))
        for j in range(LANES // HEAD_DIM):
            s, gp = part(s_all, j, 1) * (SCALE * LOG2E) + bias, part(gp_all, j, 1)
            top = jnp.max(s, axis=0, keepdims=True)
            e = jnp.exp2(s - top)
            h = first + j
            top_ref[h : h + 1, :] = top
            sum_ref[h : h + 1, :] = jnp.sum(e, axis=0, keepdims=True)
            dot_ref[h : h + 1, :] = jnp.sum(e * gp, axis=0, keepdims=True)


def near_stats_kernel(
    q_ref, g_ref, k_ref, v_ref, k_oth, v_oth, lc_ref, s2_ref, off_ref, bias_ref,
    kall_ref, vall_ref, top_ref, sum_ref, dot_ref,
):
    assemble(kall_ref, k_ref, k_oth, lc_ref.at[0], s2_ref.at[0], off_ref.at[0])
    assemble(vall_ref, v_ref, v_oth, lc_ref.at[1], s2_ref.at[1], off_ref.at[1])
    near = kall_ref.shape[0]
    partial_stats(
        q_ref, g_ref, kall_ref, vall_ref, bias_ref[0:near, :], top_ref, sum_ref, dot_ref
    )


def far_stats_kernel(
    q_ref, g_ref, off_ref, bias_ref, top_ref, sum_ref, dot_ref, st_ref, top2, sum2, dot2
):
    near = bias_ref.shape[0] - off_ref.shape[1]
    partial_stats(
        q_ref, g_ref, off_ref.at[0], off_ref.at[1], bias_ref[near:, :], top2, sum2, dot2
    )
    top = jnp.maximum(top_ref[...], top2[...])
    a, b = jnp.exp2(top_ref[...] - top), jnp.exp2(top2[...] - top)
    total = sum_ref[...] * a + sum2[...] * b
    log_total = top + jnp.log2(total)
    dot = (dot_ref[...] * a + dot2[...] * b) / total
    terms = []
    for x in (log_total, dot):
        high = x.astype(jnp.bfloat16).astype(jnp.float32)
        mid = (x - high).astype(jnp.bfloat16).astype(jnp.float32)
        terms += [high, mid, x - high - mid]
    count = sum(x.shape[0] for x in terms)
    terms.append(jnp.zeros((LANES - count, top.shape[1]), jnp.float32))
    st_ref[...] = jnp.concatenate(terms, axis=0).T.astype(jnp.bfloat16)


def query_kernel(
    q_ref, g_ref, kall_ref, vall_ref, corner_ref, near_ref, far_ref, st_ref, dq_ref
):
    heads = q_ref.shape[1] // HEAD_DIM
    near = near_ref.shape[1]
    row = lax.broadcasted_iota(jnp.int32, (LANES, LANES), 0)

    def stat_of(h):
        choose = (row == h) | (row == h + heads) | (row == h + 2 * heads)
        choose = jnp.where(choose, 1.0, 0.0).astype(jnp.bfloat16)
        return jnp.dot(st_ref[...], choose, preferred_element_type=jnp.float32)

    def wide(x, count):
        return jnp.concatenate([x] * -(-count // LANES), axis=1)[:, :count]

    per = LANES // HEAD_DIM
    for at, first in groups(q_ref.shape[1]):
        k_far = jnp.concatenate([kall_ref[near:, at], corner_ref[0, :, at]], axis=0)
        v_far = jnp.concatenate([vall_ref[near:, at], corner_ref[1, :, at]], axis=0)
        sides = (
            (kall_ref[0:near, at], vall_ref[0:near, at], near_ref[...]),
            (k_far, v_far, far_ref[...]),
        )
        qs, gs = spread(q_ref[:, at]), spread(g_ref[:, at])
        logs = [stat_of(first + j) for j in range(per)]
        dots = [stat_of(first + j + 3 * heads) for j in range(per)]
        total = jnp.zeros((q_ref.shape[0], LANES), jnp.float32)
        for kg, vg, bias in sides:
            count = kg.shape[0]
            s, gp = dot_nt(qs, kg), dot_nt(gs, vg)
            ds = []
            for j in range(per):
                p = jnp.exp2(part(s, j, 0) * (SCALE * LOG2E) + (bias - wide(logs[j], count)))
                ds.append((p * (part(gp, j, 0) - wide(dots[j], count))).astype(jnp.bfloat16))
            ds = jnp.concatenate(ds, axis=0)
            total += gather(jnp.dot(ds, kg, preferred_element_type=jnp.float32))
        dq_ref[:, at] = (total * SCALE).astype(jnp.bfloat16)


def key_sums(k_ref, v_ref, queries, grads, stats, bias, stat_rows, finish):
    heads = k_ref.shape[1] // HEAD_DIM
    row = lax.broadcasted_iota(jnp.int32, (2 * heads, LANES), 0)
    col = lax.broadcasted_iota(jnp.int32, (2 * heads, LANES), 1)
    base = jnp.where(row < heads, row, row + 2 * heads)
    choose = (col == base) | (col == base + heads) | (col == base + 2 * heads)
    choose = jnp.where(choose, 1.0, 0.0).astype(jnp.bfloat16)
    stat_rows[...] = dot_nt(choose, stats[...])
    for at, first in groups(k_ref.shape[1]):
        qg, gg = queries[:, at], grads[:, at]
        s, gp = dot_nt(spread(k_ref[:, at]), qg), dot_nt(spread(v_ref[:, at]), gg)
        p_half, ds = [], []
        for j in range(LANES // HEAD_DIM):
            h = first + j
            log_total, dot = stat_rows[h : h + 1, :], stat_rows[h + heads : h + heads + 1, :]
            p = jnp.exp2(part(s, j, 0) * (SCALE * LOG2E) + (bias - log_total))
            p_half.append(p.astype(jnp.bfloat16))
            ds.append((p * (part(gp, j, 0) - dot)).astype(jnp.bfloat16))
        dv = jnp.dot(jnp.concatenate(p_half, axis=0), gg, preferred_element_type=jnp.float32)
        dk = jnp.dot(jnp.concatenate(ds, axis=0), qg, preferred_element_type=jnp.float32)
        finish(at, gather(dk), gather(dv))


def near_key_kernel(
    k_ref, v_ref, q_ref, g_ref, q_oth, g_oth, lc_ref, s2_ref,
    st_ref, st_oth, st_lc, st_s2, bias_ref, dk_ref, dv_ref, qall, gall, stall, stat_rows,
):
    assemble(qall, q_ref, q_oth, lc_ref.at[0], s2_ref.at[0])
    assemble(gall, g_ref, g_oth, lc_ref.at[1], s2_ref.at[1])
    assemble(stall, st_ref, st_oth, st_lc, st_s2)

    def finish(at, dk, dv):
        dk_ref[:, at], dv_ref[:, at] = dk, dv

    key_sums(k_ref, v_ref, qall, gall, stall, bias_ref[...], stat_rows, finish)


def far_key_kernel(
    k_ref, v_ref, off_ref, st_off, bias_ref, dk_in, dv_in, dk_ref, dv_ref, stat_rows
):

    def finish(at, dk, dv):
        dk_ref[:, at] = ((dk_in[:, at] + dk) * SCALE).astype(jnp.bfloat16)
        dv_ref[:, at] = (dv_in[:, at] + dv).astype(jnp.bfloat16)

    key_sums(k_ref, v_ref, off_ref.at[0], off_ref.at[1], st_off, bias_ref[...], stat_rows, finish)


def shards(lat_count, lon_count, query, key, value, grad, pole_reach):
    rows, cols, width = query.shape
    lat, lon = lax.axis_index("lat"), lax.axis_index("lon")
    odd = lax.rem(lat, 2)
    even = odd == 0
    pair, around, across = routes(lat_count, lon_count)
    axes = ("lat", "lon")
    n_own, n_oth, n_strip, _, n_off, n_corner = pieces(rows, cols)
    near = n_own + n_oth + 2 * n_strip
    far = n_off + n_corner
    place = jnp.stack([lat, lon]).astype(jnp.int32)

    smem = pl.BlockSpec(memory_space=pltpu.SMEM)
    vmem = pl.BlockSpec(memory_space=pltpu.VMEM)

    def call(body, outs, operands, scratch=(), flops=1 << 10, scalars=False):
        return pl.pallas_call(
            body,
            out_shape=outs,
            in_specs=[smem] * scalars + [vmem] * (len(operands) - scalars),
            out_specs=jax.tree.map(lambda _: vmem, outs),
            scratch_shapes=scratch,
            compiler_params=pltpu.CompilerParams(vmem_limit_bytes=16 << 20),
            cost_estimate=pl.CostEstimate(flops=flops, bytes_accessed=1 << 10, transcendentals=0),
        )(*operands)

    def array(*shape, dtype=jnp.bfloat16):
        return jax.ShapeDtypeStruct(shape, dtype)

    f32 = jnp.float32
    heads = width // HEAD_DIM
    def strip_of(mine, other):
        side = [jnp.where(even, x[:, cols - RADIUS :], x[:, :RADIUS]) for x in (mine, other)]
        return jnp.concatenate([x.reshape(rows * RADIUS, -1) for x in side], axis=0)

    def edge_of(mine, even=even):
        return jnp.where(even, mine[:RADIUS], mine[rows - RADIUS :]).reshape(n_off, -1)

    def corner_of(first, second):
        count, half = RADIUS * RADIUS, n_strip // 2
        parts = [
            jnp.where(even, x[at : at + count], x[at + half - count : at + half])
            for x, at in ((first, 0), (second, half))
        ]
        parts.append(jnp.zeros((n_corner - 2 * count, first.shape[1]), first.dtype))
        return jnp.concatenate(parts, axis=0)

    def send(block, route):
        return lax.ppermute(block, axes, route)

    def flat(field):
        return field.reshape(n_own, field.shape[-1])

    def strips(mine, other):
        return jnp.stack([strip_of(a, b) for a, b in zip(mine, other)])

    def edges(mine, even=even):
        return jnp.stack([edge_of(a, even) for a in mine])

    def corners(first, second):
        return jnp.stack([corner_of(a, b) for a, b in zip(first, second)])

    key_o, value_o = send(key, pair), send(value, pair)
    kv, kv_o = (key, value), (key_o, value_o)
    kv_strip, place = lax.optimization_barrier((strips(kv, kv_o), place))
    kv_1 = send(kv_strip, around)

    reach = pole_reach.astype(f32)
    table = np.concatenate(
        [layout(rows, cols, odd, pole) for odd in (False, True) for pole in (False, True)]
    )
    bias_near, bias_far, bias_t = call(
        functools.partial(mask_kernel, rows, cols, lat_count, lon_count),
        (
            array(n_own, near, dtype=f32),
            array(n_own, far, dtype=f32),
            array(near + far, n_own, dtype=f32),
        ),
        (place, reach, reach.T, jnp.asarray(table)),
        scalars=True,
    )

    later, query_s, grad_s, bias_t = lax.optimization_barrier((even, query, grad, bias_t))
    kv_off = send(edges(kv, later), across)
    kv_2 = send(kv_1, pair)
    kv_corner = send(corners(kv_1, kv_2), across)
    query_o, grad_o = send(query_s, pair), send(grad_s, pair)
    qg, qg_o = (query, grad), (query_o, grad_o)
    qg_1 = send(strips(qg, qg_o), around)

    q, k, v, g = (flat(x) for x in (query, key, value, grad))
    stat = array(heads, n_own, dtype=f32)
    kall, vall, *near_stats = call(
        near_stats_kernel,
        (array(near + n_off, width), array(near + n_off, width), stat, stat, stat),
        (q, g, k, v, flat(key_o), flat(value_o), kv_1, kv_2, kv_off, bias_t),
    )
    stats = call(
        far_stats_kernel,
        array(n_own, LANES),
        (q, g, kv_corner, bias_t, *near_stats),
        [pltpu.VMEM((heads, n_own), f32)] * 3,
    )
    stats_grid = stats.reshape(rows, cols, LANES)
    stats_o = send(stats_grid, pair)
    qg_1, _ = lax.optimization_barrier((qg_1, stats_o))
    qg_2 = send(qg_1, pair)
    qg_beyond = jnp.concatenate([edges(qg), corners(qg_1, qg_2)], axis=1)
    st_strip, qg_beyond, stats_q = lax.optimization_barrier(
        (strip_of(stats_grid, stats_o), qg_beyond, stats)
    )
    st_1 = send(st_strip, around)
    qg_off = send(qg_beyond, across)
    d_query = call(
        query_kernel,
        array(n_own, width),
        (q, g, kall, vall, kv_corner, bias_near, bias_far, stats_q),
    )
    st_1, d_query = lax.optimization_barrier((st_1, d_query))
    st_2 = send(st_1, pair)
    st_off = send(
        jnp.concatenate([edge_of(stats_grid), corner_of(st_1, st_2)], axis=0), across
    )

    sums = array(n_own, width, dtype=f32)
    d_key, d_value = call(
        near_key_kernel,
        (sums, sums),
        (
            k, v, q, g, flat(query_o), flat(grad_o), qg_1, qg_2,
            stats, flat(stats_o), st_1, st_2, bias_near,
        ),
        [
            pltpu.VMEM((near, width), jnp.bfloat16),
            pltpu.VMEM((near, width), jnp.bfloat16),
            pltpu.VMEM((near, LANES), jnp.bfloat16),
            pltpu.VMEM((2 * heads, near), f32),
        ],
    )
    d_key, d_value = call(
        far_key_kernel,
        (array(n_own, width), array(n_own, width)),
        (k, v, qg_off, st_off, bias_far, d_key, d_value),
        [pltpu.VMEM((2 * heads, far), f32)],
    )
    shape = (rows, cols, width)
    return d_query.reshape(shape), d_key.reshape(shape), d_value.reshape(shape)


def solution(mesh):
    field = P("lat", "lon", None)
    return jax.shard_map(
        functools.partial(shards, mesh.shape["lat"], mesh.shape["lon"]),
        mesh=mesh,
        in_specs=(field, field, field, field, P()),
        out_specs=(field, field, field),
        check_vma=False,
    )
```

```python
import functools
import math

import jax
import jax.numpy as jnp
import numpy as np
from jax import lax
from jax.experimental import pallas as pl
from jax.experimental.pallas import tpu as pltpu
from jax.sharding import PartitionSpec as P

HEAD_DIM = 32
RADIUS = 6
LANES = 128
NEG = -1e30
LOG2E = 1.4426950408889634


def routes(lat_count, lon_count):
    half = lon_count // 2
    pair, around, across = [], [], []
    for i in range(lat_count):
        for j in range(lon_count):
            me = i * lon_count + j
            pair.append((me, (i ^ 1) * lon_count + j))
            step = 1 if i % 2 == 0 else -1
            around.append((me, i * lon_count + (j + step) % lon_count))
            other = i - 1 if i % 2 == 0 else i + 1
            if 0 <= other < lat_count:
                across.append((me, other * lon_count + j))
            else:
                across.append((me, i * lon_count + (j + half) % lon_count))
    return pair, around, across


def pieces(rows, cols):
    corners = 2 * RADIUS * RADIUS
    pad = -corners % 16
    strip = 2 * rows * RADIUS
    return rows * cols, rows * cols, strip, strip, RADIUS * cols, corners + pad


def layout(rows, cols, odd, pole):
    west, east = range(-RADIUS, 0), range(cols, cols + RADIUS)
    mine, other = range(0, rows), range(-rows, 0) if odd else range(rows, 2 * rows)
    beyond = range(rows, rows + RADIUS) if odd else range(-RADIUS, 0)
    if pole:
        beyond = beyond[::-1]
    sender_odd = odd if pole else not odd
    places = [(r, c) for r in range(rows) for c in range(cols)]
    places += [(r + (-rows if odd else rows), c) for r, c in places]
    first, second = (east, west) if odd else (west, east)
    for side, bands in ((first, (mine, other)), (second, (other, mine))):
        places += [(r, c) for band in bands for r in band for c in side]
    places += [(r, c) for r in beyond for c in range(cols)]
    for side in (east, west) if sender_odd else (west, east):
        places += [(r, c) for r in beyond for c in side]
    nowhere = (1 << 20, 0)
    places += [nowhere] * (sum(pieces(rows, cols)) - len(places))
    return np.array(places, np.int32).T


def mask_kernel(
    rows, cols, lat_count, lon_count, sc_ref, reach_ref, reach_t_ref, table_ref,
    near_ref, far_ref, out_t_ref,
):
    lat, lon = sc_ref[0], sc_ref[1]
    total_rows, total_cols = rows * lat_count, cols * lon_count
    odd = lax.rem(lat, 2)
    pole = jnp.where(jnp.where(odd == 0, lat, lat_count - 1 - lat) == 0, 1, 0)
    row0, col0 = lat * rows, lon * cols
    which = 2 * (2 * odd + pole)
    r_key = table_ref[pl.ds(which, 1), :]
    c_key = table_ref[pl.ds(which + 1, 1), :]
    outer = r_key.shape[1]
    g_key = r_key + row0
    turned = lax.rem(c_key + (col0 + total_cols // 2 + total_cols), total_cols)
    pick = lax.broadcasted_iota(jnp.int32, (total_cols, outer), 0) == turned
    north_key = jnp.sum(jnp.where(pick, reach_t_ref[:, 0:1], 0.0), axis=0, keepdims=True)
    south_key = jnp.sum(jnp.where(pick, reach_t_ref[:, 1:2], 0.0), axis=0, keepdims=True)
    g_f = g_key.astype(jnp.float32)
    behind_n = g_key < 0
    behind_s = g_key >= total_rows
    spare = jnp.where(
        behind_n, north_key + 1.0 + g_f, jnp.where(behind_s, south_key + total_rows - g_f, 1.0)
    )
    valid = jnp.where(spare > 0.5, 1.0, 0.0)
    n = lax.broadcasted_iota(jnp.int32, (rows * cols, 1), 0)
    shift = cols.bit_length() - 1
    r_n, c_n = lax.shift_right_logical(n, shift), n & (cols - 1)
    pick_n = lax.broadcasted_iota(jnp.int32, (rows * cols, total_cols), 1) == (c_n + col0)
    north_n = jnp.sum(jnp.where(pick_n, reach_ref[0:1, :], 0.0), axis=1, keepdims=True)
    south_n = jnp.sum(jnp.where(pick_n, reach_ref[1:2, :], 0.0), axis=1, keepdims=True)
    g_n = (r_n + row0).astype(jnp.float32)
    north_ok = jnp.where(north_n > g_n, 1.0, 0.0)
    south_ok = jnp.where(south_n > total_rows - 1 - g_n, 1.0, 0.0)
    need_n = jnp.where(behind_n, 1.0, 0.0)
    need_s = jnp.where(behind_s, 1.0, 0.0)
    near = (jnp.abs(r_key - r_n) <= RADIUS) & (jnp.abs(c_key - c_n) <= RADIUS)
    ok = jnp.where(near, 1.0, 0.0) * valid
    ok = jnp.where(need_n > north_ok, 0.0, ok)
    ok = jnp.where(need_s > south_ok, 0.0, ok)
    bias = jnp.where(ok > 0.5, 0.0, NEG)
    count = near_ref.shape[1]
    near_ref[...] = bias[:, 0:count]
    far_ref[...] = bias[:, count:]
    out_t_ref[...] = bias.T


def assemble(target, *pieces):
    at = 0
    for piece in pieces:
        target[at : at + piece.shape[0]] = piece[...]
        at += piece.shape[0]


NT = (((1,), (1,)), ((), ()))
SCALE = 1.0 / math.sqrt(HEAD_DIM)


def lanes_of(shape, j):
    lane = lax.broadcasted_iota(jnp.int32, shape, 1)
    return (lane >= j * HEAD_DIM) & (lane < (j + 1) * HEAD_DIM)


def spread(x):
    per = LANES // HEAD_DIM
    return jnp.concatenate(
        [jnp.where(lanes_of(x.shape, j), x, jnp.zeros_like(x)) for j in range(per)], axis=0
    )


def gather(x):
    per = LANES // HEAD_DIM
    count = x.shape[0] // per
    total = x[0:count]
    for j in range(1, per):
        total = jnp.where(lanes_of((count, LANES), j), x[j * count : (j + 1) * count], total)
    return total


def part(x, j, axis):
    count = x.shape[axis] // (LANES // HEAD_DIM)
    return lax.slice_in_dim(x, j * count, (j + 1) * count, axis=axis)


def groups(width):
    for g in range(width // LANES):
        yield slice(g * LANES, (g + 1) * LANES), g * (LANES // HEAD_DIM)


def dot_nt(a, b):
    return lax.dot_general(a, b, NT, preferred_element_type=jnp.float32)


def partial_stats(q_ref, g_ref, keys, values, bias, top_ref, sum_ref, dot_ref):
    for at, first in groups(q_ref.shape[1]):
        s_all = dot_nt(keys[:, at], spread(q_ref[:, at]))
        gp_all = dot_nt(values[:, at], spread(g_ref[:, at]))
        for j in range(LANES // HEAD_DIM):
            s, gp = part(s_all, j, 1) * (SCALE * LOG2E) + bias, part(gp_all, j, 1)
            top = jnp.max(s, axis=0, keepdims=True)
            e = jnp.exp2(s - top)
            h = first + j
            top_ref[h : h + 1, :] = top
            sum_ref[h : h + 1, :] = jnp.sum(e, axis=0, keepdims=True)
            dot_ref[h : h + 1, :] = jnp.sum(e * gp, axis=0, keepdims=True)


def near_stats_kernel(
    q_ref, g_ref, k_ref, v_ref, k_oth, v_oth, lc_ref, s2_ref, off_ref, bias_ref,
    kall_ref, vall_ref, top_ref, sum_ref, dot_ref,
):
    assemble(kall_ref, k_ref, k_oth, lc_ref.at[0], s2_ref.at[0], off_ref.at[0])
    assemble(vall_ref, v_ref, v_oth, lc_ref.at[1], s2_ref.at[1], off_ref.at[1])
    near = kall_ref.shape[0]
    partial_stats(
        q_ref, g_ref, kall_ref, vall_ref, bias_ref[0:near, :], top_ref, sum_ref, dot_ref
    )


def far_stats_kernel(
    q_ref, g_ref, off_ref, bias_ref, top_ref, sum_ref, dot_ref, st_ref, top2, sum2, dot2
):
    near = bias_ref.shape[0] - off_ref.shape[1]
    partial_stats(
        q_ref, g_ref, off_ref.at[0], off_ref.at[1], bias_ref[near:, :], top2, sum2, dot2
    )
    top = jnp.maximum(top_ref[...], top2[...])
    a, b = jnp.exp2(top_ref[...] - top), jnp.exp2(top2[...] - top)
    total = sum_ref[...] * a + sum2[...] * b
    log_total = top + jnp.log2(total)
    dot = (dot_ref[...] * a + dot2[...] * b) / total
    terms = []
    for x in (log_total, dot):
        high = x.astype(jnp.bfloat16).astype(jnp.float32)
        mid = (x - high).astype(jnp.bfloat16).astype(jnp.float32)
        terms += [high, mid, x - high - mid]
    count = sum(x.shape[0] for x in terms)
    terms.append(jnp.zeros((LANES - count, top.shape[1]), jnp.float32))
    st_ref[...] = jnp.concatenate(terms, axis=0).T.astype(jnp.bfloat16)


def query_kernel(
    q_ref, g_ref, kall_ref, vall_ref, corner_ref, near_ref, far_ref, st_ref, dq_ref
):
    heads = q_ref.shape[1] // HEAD_DIM
    near = near_ref.shape[1]
    row = lax.broadcasted_iota(jnp.int32, (LANES, LANES), 0)

    def stat_of(h):
        choose = (row == h) | (row == h + heads) | (row == h + 2 * heads)
        choose = jnp.where(choose, 1.0, 0.0).astype(jnp.bfloat16)
        return jnp.dot(st_ref[...], choose, preferred_element_type=jnp.float32)

    def wide(x, count):
        return jnp.concatenate([x] * -(-count // LANES), axis=1)[:, :count]

    per = LANES // HEAD_DIM
    for at, first in groups(q_ref.shape[1]):
        k_far = jnp.concatenate([kall_ref[near:, at], corner_ref[0, :, at]], axis=0)
        v_far = jnp.concatenate([vall_ref[near:, at], corner_ref[1, :, at]], axis=0)
        sides = (
            (kall_ref[0:near, at], vall_ref[0:near, at], near_ref[...]),
            (k_far, v_far, far_ref[...]),
        )
        qs, gs = spread(q_ref[:, at]), spread(g_ref[:, at])
        logs = [stat_of(first + j) for j in range(per)]
        dots = [stat_of(first + j + 3 * heads) for j in range(per)]
        total = jnp.zeros((q_ref.shape[0], LANES), jnp.float32)
        for kg, vg, bias in sides:
            count = kg.shape[0]
            s, gp = dot_nt(qs, kg), dot_nt(gs, vg)
            ds = []
            for j in range(per):
                p = jnp.exp2(part(s, j, 0) * (SCALE * LOG2E) + (bias - wide(logs[j], count)))
                ds.append((p * (part(gp, j, 0) - wide(dots[j], count))).astype(jnp.bfloat16))
            ds = jnp.concatenate(ds, axis=0)
            total += gather(jnp.dot(ds, kg, preferred_element_type=jnp.float32))
        dq_ref[:, at] = (total * SCALE).astype(jnp.bfloat16)


def key_sums(k_ref, v_ref, queries, grads, stats, bias, stat_rows, finish):
    heads = k_ref.shape[1] // HEAD_DIM
    row = lax.broadcasted_iota(jnp.int32, (2 * heads, LANES), 0)
    col = lax.broadcasted_iota(jnp.int32, (2 * heads, LANES), 1)
    base = jnp.where(row < heads, row, row + 2 * heads)
    choose = (col == base) | (col == base + heads) | (col == base + 2 * heads)
    choose = jnp.where(choose, 1.0, 0.0).astype(jnp.bfloat16)
    stat_rows[...] = dot_nt(choose, stats[...])
    for at, first in groups(k_ref.shape[1]):
        qg, gg = queries[:, at], grads[:, at]
        s, gp = dot_nt(spread(k_ref[:, at]), qg), dot_nt(spread(v_ref[:, at]), gg)
        p_half, ds = [], []
        for j in range(LANES // HEAD_DIM):
            h = first + j
            log_total, dot = stat_rows[h : h + 1, :], stat_rows[h + heads : h + heads + 1, :]
            p = jnp.exp2(part(s, j, 0) * (SCALE * LOG2E) + (bias - log_total))
            p_half.append(p.astype(jnp.bfloat16))
            ds.append((p * (part(gp, j, 0) - dot)).astype(jnp.bfloat16))
        dv = jnp.dot(jnp.concatenate(p_half, axis=0), gg, preferred_element_type=jnp.float32)
        dk = jnp.dot(jnp.concatenate(ds, axis=0), qg, preferred_element_type=jnp.float32)
        finish(at, gather(dk), gather(dv))


def near_key_kernel(
    k_ref, v_ref, q_ref, g_ref, q_oth, g_oth, lc_ref, s2_ref,
    st_ref, st_oth, st_lc, st_s2, bias_ref, dk_ref, dv_ref, qall, gall, stall, stat_rows,
):
    assemble(qall, q_ref, q_oth, lc_ref.at[0], s2_ref.at[0])
    assemble(gall, g_ref, g_oth, lc_ref.at[1], s2_ref.at[1])
    assemble(stall, st_ref, st_oth, st_lc, st_s2)

    def finish(at, dk, dv):
        dk_ref[:, at], dv_ref[:, at] = dk, dv

    key_sums(k_ref, v_ref, qall, gall, stall, bias_ref[...], stat_rows, finish)


def far_key_kernel(
    k_ref, v_ref, off_ref, st_off, bias_ref, dk_in, dv_in, dk_ref, dv_ref, stat_rows
):

    def finish(at, dk, dv):
        dk_ref[:, at] = ((dk_in[:, at] + dk) * SCALE).astype(jnp.bfloat16)
        dv_ref[:, at] = (dv_in[:, at] + dv).astype(jnp.bfloat16)

    key_sums(k_ref, v_ref, off_ref.at[0], off_ref.at[1], st_off, bias_ref[...], stat_rows, finish)


def shards(lat_count, lon_count, query, key, value, grad, pole_reach):
    rows, cols, width = query.shape
    lat, lon = lax.axis_index("lat"), lax.axis_index("lon")
    odd = lax.rem(lat, 2)
    even = odd == 0
    pair, around, across = routes(lat_count, lon_count)
    axes = ("lat", "lon")
    n_own, n_oth, n_strip, _, n_off, n_corner = pieces(rows, cols)
    near = n_own + n_oth + 2 * n_strip
    far = n_off + n_corner
    place = jnp.stack([lat, lon]).astype(jnp.int32)

    smem = pl.BlockSpec(memory_space=pltpu.SMEM)
    vmem = pl.BlockSpec(memory_space=pltpu.VMEM)

    def call(body, outs, operands, scratch=(), flops=1 << 10, scalars=False):
        return pl.pallas_call(
            body,
            out_shape=outs,
            in_specs=[smem] * scalars + [vmem] * (len(operands) - scalars),
            out_specs=jax.tree.map(lambda _: vmem, outs),
            scratch_shapes=scratch,
            compiler_params=pltpu.CompilerParams(vmem_limit_bytes=16 << 20),
            cost_estimate=pl.CostEstimate(flops=flops, bytes_accessed=1 << 10, transcendentals=0),
        )(*operands)

    def array(*shape, dtype=jnp.bfloat16):
        return jax.ShapeDtypeStruct(shape, dtype)

    f32 = jnp.float32
    heads = width // HEAD_DIM
    def strip_of(mine, other, even=even):
        side = [jnp.where(even, x[:, cols - RADIUS :], x[:, :RADIUS]) for x in (mine, other)]
        return jnp.concatenate([x.reshape(rows * RADIUS, -1) for x in side], axis=0)

    def edge_of(mine, even=even):
        return jnp.where(even, mine[:RADIUS], mine[rows - RADIUS :]).reshape(n_off, -1)

    def corner_of(first, second):
        count, half = RADIUS * RADIUS, n_strip // 2
        parts = [
            jnp.where(even, x[at : at + count], x[at + half - count : at + half])
            for x, at in ((first, 0), (second, half))
        ]
        parts.append(jnp.zeros((n_corner - 2 * count, first.shape[1]), first.dtype))
        return jnp.concatenate(parts, axis=0)

    def send(block, route):
        return lax.ppermute(block, axes, route)

    def flat(field):
        return field.reshape(n_own, field.shape[-1])

    def strips(mine, other, even=even):
        return jnp.stack([strip_of(a, b, even) for a, b in zip(mine, other)])

    def edges(mine, even=even):
        return jnp.stack([edge_of(a, even) for a in mine])

    def corners(first, second):
        return jnp.stack([corner_of(a, b) for a, b in zip(first, second)])

    key_o, value_o = send(key, pair), send(value, pair)
    kv, kv_o = (key, value), (key_o, value_o)
    query_o, grad_o = send(query, pair), send(grad, pair)
    qg, qg_o = (query, grad), (query_o, grad_o)
    kv_strip = strips(kv, kv_o)
    later, _ = lax.optimization_barrier((even, kv_strip))
    kv_1 = send(kv_strip, around)
    kv_off = send(edges(kv, later), across)
    qg_1 = send(strips(qg, qg_o, later), around)
    kv_2 = send(kv_1, pair)
    kv_last = corners(kv_1, kv_2)
    kv_corner = send(kv_last, across)
    qg_1, place, _ = lax.optimization_barrier((qg_1, place, kv_last))
    reach = pole_reach.astype(f32)
    table = np.concatenate(
        [layout(rows, cols, odd, pole) for odd in (False, True) for pole in (False, True)]
    )
    bias_near, bias_far, bias_t = call(
        functools.partial(mask_kernel, rows, cols, lat_count, lon_count),
        (
            array(n_own, near, dtype=f32),
            array(n_own, far, dtype=f32),
            array(near + far, n_own, dtype=f32),
        ),
        (place, reach, reach.T, jnp.asarray(table)),
        scalars=True,
    )

    qg_2 = send(qg_1, pair)
    qg_beyond = jnp.concatenate([edges(qg, later), corners(qg_1, qg_2)], axis=1)
    bias_t, qg_beyond = lax.optimization_barrier((bias_t, qg_beyond))

    q, k, v, g = (flat(x) for x in (query, key, value, grad))
    stat = array(heads, n_own, dtype=f32)
    kall, vall, *near_stats = call(
        near_stats_kernel,
        (array(near + n_off, width), array(near + n_off, width), stat, stat, stat),
        (q, g, k, v, flat(key_o), flat(value_o), kv_1, kv_2, kv_off, bias_t),
    )
    stats = call(
        far_stats_kernel,
        array(n_own, LANES),
        (q, g, kv_corner, bias_t, *near_stats),
        [pltpu.VMEM((heads, n_own), f32)] * 3,
    )
    stats_grid = stats.reshape(rows, cols, LANES)
    stats_o = send(stats_grid, pair)
    st_strip, qg_beyond, stats_q = lax.optimization_barrier(
        (strip_of(stats_grid, stats_o), qg_beyond, stats)
    )
    st_1 = send(st_strip, around)
    qg_off = send(qg_beyond, across)
    d_query = call(
        query_kernel,
        array(n_own, width),
        (q, g, kall, vall, kv_corner, bias_near, bias_far, stats_q),
    )
    st_1, d_query = lax.optimization_barrier((st_1, d_query))
    st_2 = send(st_1, pair)
    st_off = send(
        jnp.concatenate([edge_of(stats_grid), corner_of(st_1, st_2)], axis=0), across
    )

    sums = array(n_own, width, dtype=f32)
    d_key, d_value = call(
        near_key_kernel,
        (sums, sums),
        (
            k, v, q, g, flat(query_o), flat(grad_o), qg_1, qg_2,
            stats, flat(stats_o), st_1, st_2, bias_near,
        ),
        [
            pltpu.VMEM((near, width), jnp.bfloat16),
            pltpu.VMEM((near, width), jnp.bfloat16),
            pltpu.VMEM((near, LANES), jnp.bfloat16),
            pltpu.VMEM((2 * heads, near), f32),
        ],
    )
    d_key, d_value = call(
        far_key_kernel,
        (array(n_own, width), array(n_own, width)),
        (k, v, qg_off, st_off, bias_far, d_key, d_value),
        [pltpu.VMEM((2 * heads, far), f32)],
    )
    shape = (rows, cols, width)
    return d_query.reshape(shape), d_key.reshape(shape), d_value.reshape(shape)


def solution(mesh):
    field = P("lat", "lon", None)
    return jax.shard_map(
        functools.partial(shards, mesh.shape["lat"], mesh.shape["lon"]),
        mesh=mesh,
        in_specs=(field, field, field, field, P()),
        out_specs=(field, field, field),
        check_vma=False,
    )
```

```python
import functools
import math

import jax
import jax.numpy as jnp
import numpy as np
from jax import lax
from jax.experimental import pallas as pl
from jax.experimental.pallas import tpu as pltpu
from jax.sharding import PartitionSpec as P

HEAD_DIM = 32
RADIUS = 6
LANES = 128
NEG = -1e30
LOG2E = 1.4426950408889634


def routes(lat_count, lon_count):
    half = lon_count // 2
    pair, around, across = [], [], []
    for i in range(lat_count):
        for j in range(lon_count):
            me = i * lon_count + j
            pair.append((me, (i ^ 1) * lon_count + j))
            step = 1 if i % 2 == 0 else -1
            around.append((me, i * lon_count + (j + step) % lon_count))
            other = i - 1 if i % 2 == 0 else i + 1
            if 0 <= other < lat_count:
                across.append((me, other * lon_count + j))
            else:
                across.append((me, i * lon_count + (j + half) % lon_count))
    return pair, around, across


def pieces(rows, cols):
    corners = 2 * RADIUS * RADIUS
    pad = -corners % 16
    strip = 2 * rows * RADIUS
    return rows * cols, rows * cols, strip, strip, RADIUS * cols, corners + pad


def layout(rows, cols, odd, pole):
    west, east = range(-RADIUS, 0), range(cols, cols + RADIUS)
    mine, other = range(0, rows), range(-rows, 0) if odd else range(rows, 2 * rows)
    beyond = range(rows, rows + RADIUS) if odd else range(-RADIUS, 0)
    if pole:
        beyond = beyond[::-1]
    sender_odd = odd if pole else not odd
    places = [(r, c) for r in range(rows) for c in range(cols)]
    places += [(r + (-rows if odd else rows), c) for r, c in places]
    first, second = (east, west) if odd else (west, east)
    for side, bands in ((first, (mine, other)), (second, (other, mine))):
        places += [(r, c) for band in bands for r in band for c in side]
    places += [(r, c) for r in beyond for c in range(cols)]
    for side in (east, west) if sender_odd else (west, east):
        places += [(r, c) for r in beyond for c in side]
    nowhere = (1 << 20, 0)
    places += [nowhere] * (sum(pieces(rows, cols)) - len(places))
    return np.array(places, np.int32).T


def mask_kernel(
    rows, cols, lat_count, lon_count, sc_ref, reach_hbm, table_hbm,
    near_ref, far_ref, out_t_ref, reach_vm, table_ref, sems,
):
    copies = [
        pltpu.make_async_copy(reach_hbm, reach_vm, sems.at[0]),
        pltpu.make_async_copy(table_hbm, table_ref, sems.at[1]),
    ]
    for copy in copies:
        copy.start()
    for copy in copies:
        copy.wait()
    reach = reach_vm[...].astype(jnp.float32)
    lat, lon = sc_ref[0], sc_ref[1]
    total_rows, total_cols = rows * lat_count, cols * lon_count
    odd = lax.rem(lat, 2)
    pole = jnp.where(jnp.where(odd == 0, lat, lat_count - 1 - lat) == 0, 1, 0)
    row0, col0 = lat * rows, lon * cols
    which = 2 * (2 * odd + pole)
    r_key = table_ref[pl.ds(which, 1), :]
    c_key = table_ref[pl.ds(which + 1, 1), :]
    outer = r_key.shape[1]
    g_key = r_key + row0
    turned = lax.rem(c_key + (col0 + total_cols // 2 + total_cols), total_cols)
    pick = lax.broadcasted_iota(jnp.int32, (total_cols, outer), 0) == turned
    pick = jnp.where(pick, 1.0, 0.0)
    key_reach = jnp.dot(reach, pick, preferred_element_type=jnp.float32)
    north_key, south_key = key_reach[0:1], key_reach[1:2]
    g_f = g_key.astype(jnp.float32)
    behind_n = g_key < 0
    behind_s = g_key >= total_rows
    spare = jnp.where(
        behind_n, north_key + 1.0 + g_f, jnp.where(behind_s, south_key + total_rows - g_f, 1.0)
    )
    valid = jnp.where(spare > 0.5, 1.0, 0.0)
    n = lax.broadcasted_iota(jnp.int32, (rows * cols, 1), 0)
    shift = cols.bit_length() - 1
    r_n, c_n = lax.shift_right_logical(n, shift), n & (cols - 1)
    pick_n = lax.broadcasted_iota(jnp.int32, (rows * cols, total_cols), 1) == (c_n + col0)
    north_n = jnp.sum(jnp.where(pick_n, reach[0:1, :], 0.0), axis=1, keepdims=True)
    south_n = jnp.sum(jnp.where(pick_n, reach[1:2, :], 0.0), axis=1, keepdims=True)
    g_n = (r_n + row0).astype(jnp.float32)
    north_ok = jnp.where(north_n > g_n, 1.0, 0.0)
    south_ok = jnp.where(south_n > total_rows - 1 - g_n, 1.0, 0.0)
    need_n = jnp.where(behind_n, 1.0, 0.0)
    need_s = jnp.where(behind_s, 1.0, 0.0)
    near = (jnp.abs(r_key - r_n) <= RADIUS) & (jnp.abs(c_key - c_n) <= RADIUS)
    ok = jnp.where(near, 1.0, 0.0) * valid
    ok = jnp.where(need_n > north_ok, 0.0, ok)
    ok = jnp.where(need_s > south_ok, 0.0, ok)
    bias = jnp.where(ok > 0.5, 0.0, NEG)
    count = near_ref.shape[1]
    near_ref[...] = bias[:, 0:count]
    far_ref[...] = bias[:, count:]
    out_t_ref[...] = bias.T


def assemble(target, *pieces):
    at = 0
    for piece in pieces:
        target[at : at + piece.shape[0]] = piece[...]
        at += piece.shape[0]


NT = (((1,), (1,)), ((), ()))
SCALE = 1.0 / math.sqrt(HEAD_DIM)


def lanes_of(shape, j):
    lane = lax.broadcasted_iota(jnp.int32, shape, 1)
    return (lane >= j * HEAD_DIM) & (lane < (j + 1) * HEAD_DIM)


def spread(x):
    per = LANES // HEAD_DIM
    return jnp.concatenate(
        [jnp.where(lanes_of(x.shape, j), x, jnp.zeros_like(x)) for j in range(per)], axis=0
    )


def gather(x):
    per = LANES // HEAD_DIM
    count = x.shape[0] // per
    total = x[0:count]
    for j in range(1, per):
        total = jnp.where(lanes_of((count, LANES), j), x[j * count : (j + 1) * count], total)
    return total


def part(x, j, axis):
    count = x.shape[axis] // (LANES // HEAD_DIM)
    return lax.slice_in_dim(x, j * count, (j + 1) * count, axis=axis)


def groups(width):
    for g in range(width // LANES):
        yield slice(g * LANES, (g + 1) * LANES), g * (LANES // HEAD_DIM)


def dot_nt(a, b):
    return lax.dot_general(a, b, NT, preferred_element_type=jnp.float32)


def partial_stats(q_ref, g_ref, keys, values, bias, top_ref, sum_ref, dot_ref):
    for at, first in groups(q_ref.shape[1]):
        s_all = dot_nt(keys[:, at], spread(q_ref[:, at]))
        gp_all = dot_nt(values[:, at], spread(g_ref[:, at]))
        for j in range(LANES // HEAD_DIM):
            s, gp = part(s_all, j, 1) * (SCALE * LOG2E) + bias, part(gp_all, j, 1)
            top = jnp.max(s, axis=0, keepdims=True)
            e = jnp.exp2(s - top)
            h = first + j
            top_ref[h : h + 1, :] = top
            sum_ref[h : h + 1, :] = jnp.sum(e, axis=0, keepdims=True)
            dot_ref[h : h + 1, :] = jnp.sum(e * gp, axis=0, keepdims=True)


def near_stats_kernel(
    q_ref, g_ref, k_ref, v_ref, k_oth, v_oth, lc_ref, s2_ref, bias_ref,
    kall_ref, vall_ref, top_ref, sum_ref, dot_ref,
):
    assemble(kall_ref, k_ref, k_oth, lc_ref.at[0], s2_ref.at[0])
    assemble(vall_ref, v_ref, v_oth, lc_ref.at[1], s2_ref.at[1])
    near = kall_ref.shape[0]
    partial_stats(
        q_ref, g_ref, kall_ref, vall_ref, bias_ref[0:near, :], top_ref, sum_ref, dot_ref
    )


def far_stats_kernel(
    q_ref, g_ref, off_ref, corner_ref, bias_ref, top_ref, sum_ref, dot_ref,
    st_ref, kall_ref, vall_ref, top2, sum2, dot2,
):
    assemble(kall_ref, off_ref.at[0], corner_ref.at[0])
    assemble(vall_ref, off_ref.at[1], corner_ref.at[1])
    near = bias_ref.shape[0] - kall_ref.shape[0]
    partial_stats(q_ref, g_ref, kall_ref, vall_ref, bias_ref[near:, :], top2, sum2, dot2)
    top = jnp.maximum(top_ref[...], top2[...])
    a, b = jnp.exp2(top_ref[...] - top), jnp.exp2(top2[...] - top)
    total = sum_ref[...] * a + sum2[...] * b
    log_total = top + jnp.log2(total)
    dot = (dot_ref[...] * a + dot2[...] * b) / total
    terms = []
    for x in (log_total, dot):
        high = x.astype(jnp.bfloat16).astype(jnp.float32)
        mid = (x - high).astype(jnp.bfloat16).astype(jnp.float32)
        terms += [high, mid, x - high - mid]
    count = sum(x.shape[0] for x in terms)
    terms.append(jnp.zeros((LANES - count, top.shape[1]), jnp.float32))
    st_ref[...] = jnp.concatenate(terms, axis=0).T.astype(jnp.bfloat16)


def query_kernel(
    q_ref, g_ref, k_near, v_near, k_far, v_far, bias_near, bias_far, st_ref, dq_ref
):
    heads = q_ref.shape[1] // HEAD_DIM
    per = LANES // HEAD_DIM
    row = lax.broadcasted_iota(jnp.int32, (LANES, LANES), 0)
    sides = ((k_near, v_near, bias_near), (k_far, v_far, bias_far))

    def stat_of(h):
        choose = (row == h) | (row == h + heads) | (row == h + 2 * heads)
        choose = jnp.where(choose, 1.0, 0.0).astype(jnp.bfloat16)
        return jnp.dot(st_ref[...], choose, preferred_element_type=jnp.float32)

    def wide(x, count):
        return jnp.concatenate([x] * -(-count // LANES), axis=1)[:, :count]

    for at, first in groups(q_ref.shape[1]):
        qs, gs = spread(q_ref[:, at]), spread(g_ref[:, at])
        logs = [stat_of(first + j) for j in range(per)]
        dots = [stat_of(first + j + 3 * heads) for j in range(per)]
        total = jnp.zeros((q_ref.shape[0], LANES), jnp.float32)
        for keys, values, bias in sides:
            kg, vg = keys[:, at], values[:, at]
            count = kg.shape[0]
            s, gp = dot_nt(qs, kg), dot_nt(gs, vg)
            ds = []
            for j in range(per):
                p = jnp.exp2(part(s, j, 0) * (SCALE * LOG2E) + (bias[...] - wide(logs[j], count)))
                ds.append((p * (part(gp, j, 0) - wide(dots[j], count))).astype(jnp.bfloat16))
            ds = jnp.concatenate(ds, axis=0)
            total += gather(jnp.dot(ds, kg, preferred_element_type=jnp.float32))
        dq_ref[:, at] = (total * SCALE).astype(jnp.bfloat16)


def key_sums(k_ref, v_ref, queries, grads, stats, bias, stat_rows, finish):
    heads = k_ref.shape[1] // HEAD_DIM
    row = lax.broadcasted_iota(jnp.int32, (2 * heads, LANES), 0)
    col = lax.broadcasted_iota(jnp.int32, (2 * heads, LANES), 1)
    base = jnp.where(row < heads, row, row + 2 * heads)
    choose = (col == base) | (col == base + heads) | (col == base + 2 * heads)
    choose = jnp.where(choose, 1.0, 0.0).astype(jnp.bfloat16)
    stat_rows[...] = dot_nt(choose, stats[...])
    for at, first in groups(k_ref.shape[1]):
        qg, gg = queries[:, at], grads[:, at]
        s, gp = dot_nt(spread(k_ref[:, at]), qg), dot_nt(spread(v_ref[:, at]), gg)
        p_half, ds = [], []
        for j in range(LANES // HEAD_DIM):
            h = first + j
            log_total, dot = stat_rows[h : h + 1, :], stat_rows[h + heads : h + heads + 1, :]
            p = jnp.exp2(part(s, j, 0) * (SCALE * LOG2E) + (bias - log_total))
            p_half.append(p.astype(jnp.bfloat16))
            ds.append((p * (part(gp, j, 0) - dot)).astype(jnp.bfloat16))
        dv = jnp.dot(jnp.concatenate(p_half, axis=0), gg, preferred_element_type=jnp.float32)
        dk = jnp.dot(jnp.concatenate(ds, axis=0), qg, preferred_element_type=jnp.float32)
        finish(at, gather(dk), gather(dv))


def near_key_kernel(
    k_ref, v_ref, q_ref, g_ref, q_oth, g_oth, lc_ref, s2_ref,
    st_ref, st_oth, st_lc, st_s2, bias_ref, dk_ref, dv_ref, qall, gall, stall, stat_rows,
):
    assemble(qall, q_ref, q_oth, lc_ref.at[0], s2_ref.at[0])
    assemble(gall, g_ref, g_oth, lc_ref.at[1], s2_ref.at[1])
    assemble(stall, st_ref, st_oth, st_lc, st_s2)

    def finish(at, dk, dv):
        dk_ref[:, at], dv_ref[:, at] = dk, dv

    key_sums(k_ref, v_ref, qall, gall, stall, bias_ref[...], stat_rows, finish)


def far_key_kernel(
    k_ref, v_ref, off_ref, st_off, bias_ref, dk_in, dv_in, dk_ref, dv_ref, stat_rows
):

    def finish(at, dk, dv):
        dk_ref[:, at] = ((dk_in[:, at] + dk) * SCALE).astype(jnp.bfloat16)
        dv_ref[:, at] = (dv_in[:, at] + dv).astype(jnp.bfloat16)

    key_sums(k_ref, v_ref, off_ref.at[0], off_ref.at[1], st_off, bias_ref[...], stat_rows, finish)


def shards(lat_count, lon_count, query, key, value, grad, pole_reach):
    rows, cols, width = query.shape
    lat, lon = lax.axis_index("lat"), lax.axis_index("lon")
    odd = lax.rem(lat, 2)
    even = odd == 0
    pair, around, across = routes(lat_count, lon_count)
    axes = ("lat", "lon")
    n_own, n_oth, n_strip, _, n_off, n_corner = pieces(rows, cols)
    near = n_own + n_oth + 2 * n_strip
    far = n_off + n_corner
    place = jnp.stack([lat, lon]).astype(jnp.int32)

    smem = pl.BlockSpec(memory_space=pltpu.SMEM)
    vmem = pl.BlockSpec(memory_space=pltpu.VMEM)

    def call(body, outs, operands, scratch=(), flops=1 << 10, scalars=False, space=pltpu.VMEM):
        return pl.pallas_call(
            body,
            out_shape=outs,
            in_specs=[smem] * scalars
            + [pl.BlockSpec(memory_space=space)] * (len(operands) - scalars),
            out_specs=jax.tree.map(lambda _: vmem, outs),
            scratch_shapes=scratch,
            compiler_params=pltpu.CompilerParams(vmem_limit_bytes=16 << 20),
            cost_estimate=pl.CostEstimate(flops=flops, bytes_accessed=1 << 10, transcendentals=0),
        )(*operands)

    def array(*shape, dtype=jnp.bfloat16):
        return jax.ShapeDtypeStruct(shape, dtype)

    f32 = jnp.float32
    heads = width // HEAD_DIM
    def strip_of(mine, other):
        side = [jnp.where(even, x[:, cols - RADIUS :], x[:, :RADIUS]) for x in (mine, other)]
        return jnp.concatenate([x.reshape(rows * RADIUS, -1) for x in side], axis=0)

    def edge_of(mine):
        return jnp.where(even, mine[:RADIUS], mine[rows - RADIUS :]).reshape(n_off, -1)

    def corner_of(first, second):
        count, half = RADIUS * RADIUS, n_strip // 2
        parts = [
            jnp.where(even, x[at : at + count], x[at + half - count : at + half])
            for x, at in ((first, 0), (second, half))
        ]
        parts.append(jnp.zeros((n_corner - 2 * count, first.shape[1]), first.dtype))
        return jnp.concatenate(parts, axis=0)

    def send(block, route):
        return lax.ppermute(block, axes, route)

    def flat(field):
        return field.reshape(n_own, field.shape[-1])

    def strips(mine, other):
        return jnp.stack([strip_of(a, b) for a, b in zip(mine, other)])

    def edges(mine):
        return jnp.stack([edge_of(a) for a in mine])

    def corners(first, second):
        return jnp.stack([corner_of(a, b) for a, b in zip(first, second)])

    key_o, value_o = send(key, pair), send(value, pair)
    query_o, grad_o = send(query, pair), send(grad, pair)
    mine = lax.optimization_barrier(jnp.stack([key, value, query, grad]))
    kv_strip = strips(mine[:2], (key_o, value_o))
    later, _ = lax.optimization_barrier((mine, kv_strip))
    kv_edge = edges(later[:2])
    kv_1 = send(kv_strip, around)
    kv_off = send(kv_edge, across)
    qg_1 = send(strips(later[2:], (query_o, grad_o)), around)
    kv_2 = send(kv_1, pair)
    kv_last = corners(kv_1, kv_2)
    kv_corner = send(kv_last, across)
    qg_1, place, pole_reach, _ = lax.optimization_barrier((qg_1, place, pole_reach, kv_last))
    table = np.concatenate(
        [layout(rows, cols, odd, pole) for odd in (False, True) for pole in (False, True)]
    )
    bias_near, bias_far, bias_t = call(
        functools.partial(mask_kernel, rows, cols, lat_count, lon_count),
        (
            array(n_own, near, dtype=f32),
            array(n_own, far, dtype=f32),
            array(near + far, n_own, dtype=f32),
        ),
        (place, pole_reach, jnp.asarray(table)),
        [
            pltpu.VMEM(pole_reach.shape, jnp.int32),
            pltpu.VMEM(table.shape, jnp.int32),
            pltpu.SemaphoreType.DMA((2,)),
        ],
        scalars=True,
        space=pltpu.HBM,
    )

    qg_2 = send(qg_1, pair)
    qg_beyond = jnp.concatenate([edges(later[2:]), corners(qg_1, qg_2)], axis=1)
    bias_t, qg_beyond = lax.optimization_barrier((bias_t, qg_beyond))

    k, v, q, g = (flat(x) for x in mine)
    stat = array(heads, n_own, dtype=f32)
    k_near, v_near, *near_stats = call(
        near_stats_kernel,
        (array(near, width), array(near, width), stat, stat, stat),
        (q, g, k, v, flat(key_o), flat(value_o), kv_1, kv_2, bias_t),
    )
    stats, k_far, v_far = call(
        far_stats_kernel,
        (array(n_own, LANES), array(far, width), array(far, width)),
        (q, g, kv_off, kv_corner, bias_t, *near_stats),
        [pltpu.VMEM((heads, n_own), f32)] * 3,
    )
    stats_grid = stats.reshape(rows, cols, LANES)
    stats_o = send(stats_grid, pair)
    st_strip, qg_beyond, stats_q = lax.optimization_barrier(
        (strip_of(stats_grid, stats_o), qg_beyond, stats)
    )
    st_1 = send(st_strip, around)
    qg_off = send(qg_beyond, across)
    sums = array(n_own, width, dtype=f32)
    d_query = call(
        query_kernel,
        array(n_own, width),
        (q, g, k_near, v_near, k_far, v_far, bias_near, bias_far, stats_q),
    )
    st_1, d_query = lax.optimization_barrier((st_1, d_query))
    st_2 = send(st_1, pair)
    st_off = send(
        jnp.concatenate([edge_of(stats_grid), corner_of(st_1, st_2)], axis=0), across
    )

    d_key, d_value = call(
        near_key_kernel,
        (sums, sums),
        (
            k, v, q, g, flat(query_o), flat(grad_o), qg_1, qg_2,
            stats, flat(stats_o), st_1, st_2, bias_near,
        ),
        [
            pltpu.VMEM((near, width), jnp.bfloat16),
            pltpu.VMEM((near, width), jnp.bfloat16),
            pltpu.VMEM((near, LANES), jnp.bfloat16),
            pltpu.VMEM((2 * heads, near), f32),
        ],
    )
    d_key, d_value = call(
        far_key_kernel,
        (array(n_own, width), array(n_own, width)),
        (k, v, qg_off, st_off, bias_far, d_key, d_value),
        [pltpu.VMEM((2 * heads, far), f32)],
    )
    shape = (rows, cols, width)
    return d_query.reshape(shape), d_key.reshape(shape), d_value.reshape(shape)


def solution(mesh):
    field = P("lat", "lon", None)
    return jax.shard_map(
        functools.partial(shards, mesh.shape["lat"], mesh.shape["lon"]),
        mesh=mesh,
        in_specs=(field, field, field, field, P()),
        out_specs=(field, field, field),
        check_vma=False,
    )
```

```python
import functools
import math

import jax
import jax.numpy as jnp
import numpy as np
from jax import lax
from jax.experimental import pallas as pl
from jax.experimental.pallas import tpu as pltpu
from jax.sharding import PartitionSpec as P

HEAD_DIM = 32
RADIUS = 6
LANES = 128
NEG = -1e30
LOG2E = 1.4426950408889634


def routes(lat_count, lon_count):
    half = lon_count // 2
    pair, around, across = [], [], []
    for i in range(lat_count):
        for j in range(lon_count):
            me = i * lon_count + j
            pair.append((me, (i ^ 1) * lon_count + j))
            step = 1 if i % 2 == 0 else -1
            around.append((me, i * lon_count + (j + step) % lon_count))
            other = i - 1 if i % 2 == 0 else i + 1
            if 0 <= other < lat_count:
                across.append((me, other * lon_count + j))
            else:
                across.append((me, i * lon_count + (j + half) % lon_count))
    return pair, around, across


def pieces(rows, cols):
    corners = 2 * RADIUS * RADIUS
    pad = -corners % 8
    strip = 2 * rows * RADIUS
    return rows * cols, rows * cols, strip, strip, RADIUS * cols, corners + pad


def layout(rows, cols, odd, pole):
    west, east = range(-RADIUS, 0), range(cols, cols + RADIUS)
    mine, other = range(0, rows), range(-rows, 0) if odd else range(rows, 2 * rows)
    beyond = range(rows, rows + RADIUS) if odd else range(-RADIUS, 0)
    if pole:
        beyond = beyond[::-1]
    sender_odd = odd if pole else not odd
    places = [(r, c) for r in range(rows) for c in range(cols)]
    places += [(r + (-rows if odd else rows), c) for r, c in places]
    first, second = (east, west) if odd else (west, east)
    for side, bands in ((first, (mine, other)), (second, (other, mine))):
        places += [(r, c) for band in bands for r in band for c in side]
    places += [(r, c) for r in beyond for c in range(cols)]
    for side in (east, west) if sender_odd else (west, east):
        places += [(r, c) for r in beyond for c in side]
    nowhere = (1 << 20, 0)
    places += [nowhere] * (sum(pieces(rows, cols)) - len(places))
    return np.array(places, np.int32).T


def mask_kernel(
    rows, cols, lat_count, lon_count, sc_ref, reach_hbm, table_hbm,
    near_ref, far_ref, out_t_ref, reach_vm, table_ref, sems,
):
    copies = [
        pltpu.make_async_copy(reach_hbm, reach_vm, sems.at[0]),
        pltpu.make_async_copy(table_hbm, table_ref, sems.at[1]),
    ]
    for copy in copies:
        copy.start()
    for copy in copies:
        copy.wait()
    reach = reach_vm[...].astype(jnp.float32)
    lat, lon = sc_ref[0], sc_ref[1]
    total_rows, total_cols = rows * lat_count, cols * lon_count
    odd = lax.rem(lat, 2)
    pole = jnp.where(jnp.where(odd == 0, lat, lat_count - 1 - lat) == 0, 1, 0)
    row0, col0 = lat * rows, lon * cols
    which = 2 * (2 * odd + pole)
    r_key = table_ref[pl.ds(which, 1), :]
    c_key = table_ref[pl.ds(which + 1, 1), :]
    outer = r_key.shape[1]
    g_key = r_key + row0
    turned = lax.rem(c_key + (col0 + total_cols // 2 + total_cols), total_cols)
    pick = lax.broadcasted_iota(jnp.int32, (total_cols, outer), 0) == turned
    pick = jnp.where(pick, 1.0, 0.0)
    key_reach = jnp.dot(reach, pick, preferred_element_type=jnp.float32)
    north_key, south_key = key_reach[0:1], key_reach[1:2]
    g_f = g_key.astype(jnp.float32)
    behind_n = g_key < 0
    behind_s = g_key >= total_rows
    spare = jnp.where(
        behind_n, north_key + 1.0 + g_f, jnp.where(behind_s, south_key + total_rows - g_f, 1.0)
    )
    valid = jnp.where(spare > 0.5, 1.0, 0.0)
    n = lax.broadcasted_iota(jnp.int32, (rows * cols, 1), 0)
    shift = cols.bit_length() - 1
    r_n, c_n = lax.shift_right_logical(n, shift), n & (cols - 1)
    pick_n = lax.broadcasted_iota(jnp.int32, (rows * cols, total_cols), 1) == (c_n + col0)
    north_n = jnp.sum(jnp.where(pick_n, reach[0:1, :], 0.0), axis=1, keepdims=True)
    south_n = jnp.sum(jnp.where(pick_n, reach[1:2, :], 0.0), axis=1, keepdims=True)
    g_n = (r_n + row0).astype(jnp.float32)
    north_ok = jnp.where(north_n > g_n, 1.0, 0.0)
    south_ok = jnp.where(south_n > total_rows - 1 - g_n, 1.0, 0.0)
    need_n = jnp.where(behind_n, 1.0, 0.0)
    need_s = jnp.where(behind_s, 1.0, 0.0)
    near = (jnp.abs(r_key - r_n) <= RADIUS) & (jnp.abs(c_key - c_n) <= RADIUS)
    ok = jnp.where(near, 1.0, 0.0) * valid
    ok = jnp.where(need_n > north_ok, 0.0, ok)
    ok = jnp.where(need_s > south_ok, 0.0, ok)
    bias = jnp.where(ok > 0.5, 0.0, NEG)
    count = near_ref.shape[1]
    near_ref[...] = bias[:, 0:count]
    far_ref[...] = bias[:, count:]
    out_t_ref[...] = bias.T


def assemble(target, *pieces):
    at = 0
    for piece in pieces:
        target[at : at + piece.shape[0]] = piece[...]
        at += piece.shape[0]


NT = (((1,), (1,)), ((), ()))
SCALE = 1.0 / math.sqrt(HEAD_DIM)


def lanes_of(shape, j):
    lane = lax.broadcasted_iota(jnp.int32, shape, 1)
    return (lane >= j * HEAD_DIM) & (lane < (j + 1) * HEAD_DIM)


def spread(x):
    per = LANES // HEAD_DIM
    return jnp.concatenate(
        [jnp.where(lanes_of(x.shape, j), x, jnp.zeros_like(x)) for j in range(per)], axis=0
    )


def gather(x):
    per = LANES // HEAD_DIM
    count = x.shape[0] // per
    total = x[0:count]
    for j in range(1, per):
        total = jnp.where(lanes_of((count, LANES), j), x[j * count : (j + 1) * count], total)
    return total


def part(x, j, axis):
    count = x.shape[axis] // (LANES // HEAD_DIM)
    return lax.slice_in_dim(x, j * count, (j + 1) * count, axis=axis)


def groups(width):
    for g in range(width // LANES):
        yield slice(g * LANES, (g + 1) * LANES), g * (LANES // HEAD_DIM)


def dot_nt(a, b):
    return lax.dot_general(a, b, NT, preferred_element_type=jnp.float32)


def partial_stats(q_ref, g_ref, keys, values, bias, top_ref, sum_ref, dot_ref):
    for at, first in groups(q_ref.shape[1]):
        s_all = dot_nt(keys[:, at], spread(q_ref[:, at]))
        gp_all = dot_nt(values[:, at], spread(g_ref[:, at]))
        for j in range(LANES // HEAD_DIM):
            s, gp = part(s_all, j, 1) * (SCALE * LOG2E) + bias, part(gp_all, j, 1)
            top = jnp.max(s, axis=0, keepdims=True)
            e = jnp.exp2(s - top)
            h = first + j
            top_ref[h : h + 1, :] = top
            sum_ref[h : h + 1, :] = jnp.sum(e, axis=0, keepdims=True)
            dot_ref[h : h + 1, :] = jnp.sum(e * gp, axis=0, keepdims=True)


def near_stats_kernel(
    q_ref, g_ref, k_ref, v_ref, k_oth, v_oth, lc_ref, s2_ref, bias_ref,
    kall_ref, vall_ref, top_ref, sum_ref, dot_ref,
):
    assemble(kall_ref, k_ref, k_oth, lc_ref.at[0], s2_ref.at[0])
    assemble(vall_ref, v_ref, v_oth, lc_ref.at[1], s2_ref.at[1])
    near = kall_ref.shape[0]
    partial_stats(
        q_ref, g_ref, kall_ref, vall_ref, bias_ref[0:near, :], top_ref, sum_ref, dot_ref
    )


def far_stats_kernel(
    q_ref, g_ref, off_ref, corner_ref, bias_ref, top_ref, sum_ref, dot_ref,
    st_ref, kall_ref, vall_ref, top2, sum2, dot2,
):
    assemble(kall_ref, off_ref.at[0], corner_ref.at[0])
    assemble(vall_ref, off_ref.at[1], corner_ref.at[1])
    near = bias_ref.shape[0] - kall_ref.shape[0]
    partial_stats(q_ref, g_ref, kall_ref, vall_ref, bias_ref[near:, :], top2, sum2, dot2)
    top = jnp.maximum(top_ref[...], top2[...])
    a, b = jnp.exp2(top_ref[...] - top), jnp.exp2(top2[...] - top)
    total = sum_ref[...] * a + sum2[...] * b
    log_total = top + jnp.log2(total)
    dot = (dot_ref[...] * a + dot2[...] * b) / total
    terms = []
    for x in (log_total, dot):
        high = x.astype(jnp.bfloat16).astype(jnp.float32)
        mid = (x - high).astype(jnp.bfloat16).astype(jnp.float32)
        terms += [high, mid, x - high - mid]
    count = sum(x.shape[0] for x in terms)
    terms.append(jnp.zeros((LANES - count, top.shape[1]), jnp.float32))
    st_ref[...] = jnp.concatenate(terms, axis=0).T.astype(jnp.bfloat16)


def query_kernel(
    q_ref, g_ref, k_near, v_near, k_far, v_far, bias_near, bias_far, st_ref, *refs
):
    dq_ref = refs[-1]
    half = q_ref.shape[1] // 2
    if len(refs) > 1:
        dq_ref[:, 0:half] = refs[0][...]
    heads = q_ref.shape[1] // HEAD_DIM
    per = LANES // HEAD_DIM
    row = lax.broadcasted_iota(jnp.int32, (LANES, LANES), 0)
    sides = ((k_near, v_near, bias_near), (k_far, v_far, bias_far))

    def stat_of(h):
        choose = (row == h) | (row == h + heads) | (row == h + 2 * heads)
        choose = jnp.where(choose, 1.0, 0.0).astype(jnp.bfloat16)
        return jnp.dot(st_ref[...], choose, preferred_element_type=jnp.float32)

    def wide(x, count):
        return jnp.concatenate([x] * -(-count // LANES), axis=1)[:, :count]

    for at, first in groups(q_ref.shape[1]):
        if (at.start >= half) != (len(refs) > 1):
            continue
        qs, gs = spread(q_ref[:, at]), spread(g_ref[:, at])
        logs = [stat_of(first + j) for j in range(per)]
        dots = [stat_of(first + j + 3 * heads) for j in range(per)]
        total = jnp.zeros((q_ref.shape[0], LANES), jnp.float32)
        for keys, values, bias in sides:
            kg, vg = keys[:, at], values[:, at]
            count = kg.shape[0]
            s, gp = dot_nt(qs, kg), dot_nt(gs, vg)
            ds = []
            for j in range(per):
                p = jnp.exp2(part(s, j, 0) * (SCALE * LOG2E) + (bias[...] - wide(logs[j], count)))
                ds.append((p * (part(gp, j, 0) - wide(dots[j], count))).astype(jnp.bfloat16))
            ds = jnp.concatenate(ds, axis=0)
            total += gather(jnp.dot(ds, kg, preferred_element_type=jnp.float32))
        dq_ref[:, at] = (total * SCALE).astype(jnp.bfloat16)


def key_sums(k_ref, v_ref, queries, grads, stats, bias, stat_rows, finish):
    heads = k_ref.shape[1] // HEAD_DIM
    row = lax.broadcasted_iota(jnp.int32, (2 * heads, LANES), 0)
    col = lax.broadcasted_iota(jnp.int32, (2 * heads, LANES), 1)
    base = jnp.where(row < heads, row, row + 2 * heads)
    choose = (col == base) | (col == base + heads) | (col == base + 2 * heads)
    choose = jnp.where(choose, 1.0, 0.0).astype(jnp.bfloat16)
    stat_rows[...] = dot_nt(choose, stats[...])
    for at, first in groups(k_ref.shape[1]):
        qg, gg = queries[:, at], grads[:, at]
        s, gp = dot_nt(spread(k_ref[:, at]), qg), dot_nt(spread(v_ref[:, at]), gg)
        p_half, ds = [], []
        for j in range(LANES // HEAD_DIM):
            h = first + j
            log_total, dot = stat_rows[h : h + 1, :], stat_rows[h + heads : h + heads + 1, :]
            p = jnp.exp2(part(s, j, 0) * (SCALE * LOG2E) + (bias - log_total))
            p_half.append(p.astype(jnp.bfloat16))
            ds.append((p * (part(gp, j, 0) - dot)).astype(jnp.bfloat16))
        dv = jnp.dot(jnp.concatenate(p_half, axis=0), gg, preferred_element_type=jnp.float32)
        dk = jnp.dot(jnp.concatenate(ds, axis=0), qg, preferred_element_type=jnp.float32)
        finish(at, gather(dk), gather(dv))


def near_key_kernel(
    k_ref, v_ref, q_ref, g_ref, q_oth, g_oth, lc_ref, s2_ref,
    st_ref, st_oth, st_lc, st_s2, bias_ref, dk_ref, dv_ref, qall, gall, stall, stat_rows,
):
    assemble(qall, q_ref, q_oth, lc_ref.at[0], s2_ref.at[0])
    assemble(gall, g_ref, g_oth, lc_ref.at[1], s2_ref.at[1])
    assemble(stall, st_ref, st_oth, st_lc, st_s2)

    def finish(at, dk, dv):
        dk_ref[:, at], dv_ref[:, at] = dk, dv

    key_sums(k_ref, v_ref, qall, gall, stall, bias_ref[...], stat_rows, finish)


def far_key_kernel(
    k_ref, v_ref, off_ref, st_off, bias_ref, dk_in, dv_in, dk_ref, dv_ref, stat_rows
):

    def finish(at, dk, dv):
        dk_ref[:, at] = ((dk_in[:, at] + dk) * SCALE).astype(jnp.bfloat16)
        dv_ref[:, at] = (dv_in[:, at] + dv).astype(jnp.bfloat16)

    key_sums(k_ref, v_ref, off_ref.at[0], off_ref.at[1], st_off, bias_ref[...], stat_rows, finish)


def shards(lat_count, lon_count, query, key, value, grad, pole_reach):
    rows, cols, width = query.shape
    lat, lon = lax.axis_index("lat"), lax.axis_index("lon")
    odd = lax.rem(lat, 2)
    even = odd == 0
    pair, around, across = routes(lat_count, lon_count)
    axes = ("lat", "lon")
    n_own, n_oth, n_strip, _, n_off, n_corner = pieces(rows, cols)
    near = n_own + n_oth + 2 * n_strip
    far = n_off + n_corner
    place = jnp.stack([lat, lon]).astype(jnp.int32)

    smem = pl.BlockSpec(memory_space=pltpu.SMEM)
    vmem = pl.BlockSpec(memory_space=pltpu.VMEM)

    def call(body, outs, operands, scratch=(), flops=1 << 10, scalars=False, space=pltpu.VMEM):
        return pl.pallas_call(
            body,
            out_shape=outs,
            in_specs=[smem] * scalars
            + [pl.BlockSpec(memory_space=space)] * (len(operands) - scalars),
            out_specs=jax.tree.map(lambda _: vmem, outs),
            scratch_shapes=scratch,
            compiler_params=pltpu.CompilerParams(vmem_limit_bytes=16 << 20),
            cost_estimate=pl.CostEstimate(flops=flops, bytes_accessed=1 << 10, transcendentals=0),
        )(*operands)

    def array(*shape, dtype=jnp.bfloat16):
        return jax.ShapeDtypeStruct(shape, dtype)

    f32 = jnp.float32
    heads = width // HEAD_DIM
    def strip_of(mine, other):
        side = [jnp.where(even, x[:, cols - RADIUS :], x[:, :RADIUS]) for x in (mine, other)]
        return jnp.concatenate([x.reshape(rows * RADIUS, -1) for x in side], axis=0)

    def edge_of(mine):
        return jnp.where(even, mine[:RADIUS], mine[rows - RADIUS :]).reshape(n_off, -1)

    def corner_of(first, second):
        count, half = RADIUS * RADIUS, n_strip // 2
        parts = [
            jnp.where(even, x[at : at + count], x[at + half - count : at + half])
            for x, at in ((first, 0), (second, half))
        ]
        parts.append(jnp.zeros((n_corner - 2 * count, first.shape[1]), first.dtype))
        return jnp.concatenate(parts, axis=0)

    def send(block, route):
        return lax.ppermute(block, axes, route)

    def flat(field):
        return field.reshape(n_own, field.shape[-1])

    def strips(mine, other):
        return jnp.stack([strip_of(a, b) for a, b in zip(mine, other)])

    def edges(mine):
        return jnp.stack([edge_of(a) for a in mine])

    def corners(first, second):
        return jnp.stack([corner_of(a, b) for a, b in zip(first, second)])

    key_o, value_o = send(key, pair), send(value, pair)
    query_o, grad_o = send(query, pair), send(grad, pair)
    mine = lax.optimization_barrier(jnp.stack([key, value, query, grad]))
    kv_strip = strips(mine[:2], (key_o, value_o))
    later, _ = lax.optimization_barrier((mine, kv_strip))
    kv_edge = edges(later[:2])
    kv_1 = send(kv_strip, around)
    kv_off = send(kv_edge, across)
    qg_1 = send(strips(later[2:], (query_o, grad_o)), around)
    kv_2 = send(kv_1, pair)
    kv_last = corners(kv_1, kv_2)
    kv_corner = send(kv_last, across)
    qg_1, place, pole_reach, _ = lax.optimization_barrier((qg_1, place, pole_reach, kv_last))
    table = np.concatenate(
        [layout(rows, cols, odd, pole) for odd in (False, True) for pole in (False, True)]
    )
    bias_near, bias_far, bias_t = call(
        functools.partial(mask_kernel, rows, cols, lat_count, lon_count),
        (
            array(n_own, near, dtype=f32),
            array(n_own, far, dtype=f32),
            array(near + far, n_own, dtype=f32),
        ),
        (place, pole_reach, jnp.asarray(table)),
        [
            pltpu.VMEM(pole_reach.shape, jnp.int32),
            pltpu.VMEM(table.shape, jnp.int32),
            pltpu.SemaphoreType.DMA((2,)),
        ],
        scalars=True,
        space=pltpu.HBM,
    )

    qg_2 = send(qg_1, pair)
    qg_beyond = jnp.concatenate([edges(later[2:]), corners(qg_1, qg_2)], axis=1)
    bias_t, qg_beyond = lax.optimization_barrier((bias_t, qg_beyond))

    k, v, q, g = (flat(x) for x in mine)
    stat = array(heads, n_own, dtype=f32)
    k_near, v_near, *near_stats = call(
        near_stats_kernel,
        (array(near, width), array(near, width), stat, stat, stat),
        (q, g, k, v, flat(key_o), flat(value_o), kv_1, kv_2, bias_t),
    )
    stats, k_far, v_far = call(
        far_stats_kernel,
        (array(n_own, LANES), array(far, width), array(far, width)),
        (q, g, kv_off, kv_corner, bias_t, *near_stats),
        [pltpu.VMEM((heads, n_own), f32)] * 3,
    )
    stats_grid = stats.reshape(rows, cols, LANES)
    stats_o = send(stats_grid, pair)
    st_strip, stats_q = lax.optimization_barrier((strip_of(stats_grid, stats_o), stats))
    st_1 = send(st_strip, around)
    qg_off = send(qg_beyond, across)
    query_side = (q, g, k_near, v_near, k_far, v_far, bias_near, bias_far)
    d_query = call(query_kernel, array(n_own, width // 2), (*query_side, stats_q))
    st_1, d_query = lax.optimization_barrier((st_1, d_query))
    st_2 = send(st_1, pair)
    _, stats_q = lax.optimization_barrier((st_2, stats))
    st_off = send(
        jnp.concatenate([edge_of(stats_grid), corner_of(st_1, st_2)], axis=0), across
    )

    d_query = call(query_kernel, array(n_own, width), (*query_side, stats_q, d_query))
    d_key, d_value = call(
        near_key_kernel,
        (array(n_own, width, dtype=f32),) * 2,
        (
            k, v, q, g, flat(query_o), flat(grad_o), qg_1, qg_2,
            stats, flat(stats_o), st_1, st_2, bias_near,
        ),
        [
            pltpu.VMEM((near, width), jnp.bfloat16),
            pltpu.VMEM((near, width), jnp.bfloat16),
            pltpu.VMEM((near, LANES), jnp.bfloat16),
            pltpu.VMEM((2 * heads, near), f32),
        ],
    )
    d_key, d_value = call(
        far_key_kernel,
        (array(n_own, width), array(n_own, width)),
        (k, v, qg_off, st_off, bias_far, d_key, d_value),
        [pltpu.VMEM((2 * heads, far), f32)],
    )
    shape = (rows, cols, width)
    return d_query.reshape(shape), d_key.reshape(shape), d_value.reshape(shape)


def solution(mesh):
    field = P("lat", "lon", None)
    return jax.shard_map(
        functools.partial(shards, mesh.shape["lat"], mesh.shape["lon"]),
        mesh=mesh,
        in_specs=(field, field, field, field, P()),
        out_specs=(field, field, field),
        check_vma=False,
    )
```

```python
import functools
import math

import jax
import jax.numpy as jnp
import numpy as np
from jax import lax
from jax.experimental import pallas as pl
from jax.experimental.pallas import tpu as pltpu
from jax.sharding import PartitionSpec as P

HEAD_DIM = 32
RADIUS = 6
LANES = 128
NEG = -1e30
LOG2E = 1.4426950408889634


def routes(lat_count, lon_count):
    half = lon_count // 2
    pair, around, across = [], [], []
    for i in range(lat_count):
        for j in range(lon_count):
            me = i * lon_count + j
            pair.append((me, (i ^ 1) * lon_count + j))
            step = 1 if i % 2 == 0 else -1
            around.append((me, i * lon_count + (j + step) % lon_count))
            other = i - 1 if i % 2 == 0 else i + 1
            if 0 <= other < lat_count:
                across.append((me, other * lon_count + j))
            else:
                across.append((me, i * lon_count + (j + half) % lon_count))
    return pair, around, across


def pieces(rows, cols):
    corners = 2 * RADIUS * RADIUS
    pad = -corners % 8
    strip = 2 * rows * RADIUS
    return rows * cols, rows * cols, strip, strip, RADIUS * cols, corners + pad


def layout(rows, cols, odd, pole):
    west, east = range(-RADIUS, 0), range(cols, cols + RADIUS)
    mine, other = range(0, rows), range(-rows, 0) if odd else range(rows, 2 * rows)
    beyond = range(rows, rows + RADIUS) if odd else range(-RADIUS, 0)
    if pole:
        beyond = beyond[::-1]
    sender_odd = odd if pole else not odd
    places = [(r, c) for r in range(rows) for c in range(cols)]
    places += [(r + (-rows if odd else rows), c) for r, c in places]
    first, second = (east, west) if odd else (west, east)
    for side, bands in ((first, (mine, other)), (second, (other, mine))):
        places += [(r, c) for band in bands for r in band for c in side]
    places += [(r, c) for r in beyond for c in range(cols)]
    for side in (east, west) if sender_odd else (west, east):
        places += [(r, c) for r in beyond for c in side]
    nowhere = (1 << 20, 0)
    places += [nowhere] * (sum(pieces(rows, cols)) - len(places))
    return np.array(places, np.int32).T


def mask_kernel(
    rows, cols, lat_count, lon_count, sc_ref, reach_hbm, table_hbm,
    near_ref, far_ref, out_t_ref, reach_vm, table_ref, sems,
):
    copies = [
        pltpu.make_async_copy(reach_hbm, reach_vm, sems.at[0]),
        pltpu.make_async_copy(table_hbm, table_ref, sems.at[1]),
    ]
    for copy in copies:
        copy.start()
    for copy in copies:
        copy.wait()
    reach = reach_vm[...].astype(jnp.float32)
    lat, lon = sc_ref[0], sc_ref[1]
    total_rows, total_cols = rows * lat_count, cols * lon_count
    odd = lax.rem(lat, 2)
    pole = jnp.where(jnp.where(odd == 0, lat, lat_count - 1 - lat) == 0, 1, 0)
    row0, col0 = lat * rows, lon * cols
    which = 2 * (2 * odd + pole)
    r_key = table_ref[pl.ds(which, 1), :]
    c_key = table_ref[pl.ds(which + 1, 1), :]
    outer = r_key.shape[1]
    g_key = r_key + row0
    turned = lax.rem(c_key + (col0 + total_cols // 2 + total_cols), total_cols)
    pick = lax.broadcasted_iota(jnp.int32, (total_cols, outer), 0) == turned
    pick = jnp.where(pick, 1.0, 0.0)
    key_reach = jnp.dot(reach, pick, preferred_element_type=jnp.float32)
    north_key, south_key = key_reach[0:1], key_reach[1:2]
    g_f = g_key.astype(jnp.float32)
    behind_n = g_key < 0
    behind_s = g_key >= total_rows
    spare = jnp.where(
        behind_n, north_key + 1.0 + g_f, jnp.where(behind_s, south_key + total_rows - g_f, 1.0)
    )
    valid = jnp.where(spare > 0.5, 1.0, 0.0)
    n = lax.broadcasted_iota(jnp.int32, (rows * cols, 1), 0)
    shift = cols.bit_length() - 1
    r_n, c_n = lax.shift_right_logical(n, shift), n & (cols - 1)
    pick_n = lax.broadcasted_iota(jnp.int32, (rows * cols, total_cols), 1) == (c_n + col0)
    north_n = jnp.sum(jnp.where(pick_n, reach[0:1, :], 0.0), axis=1, keepdims=True)
    south_n = jnp.sum(jnp.where(pick_n, reach[1:2, :], 0.0), axis=1, keepdims=True)
    g_n = (r_n + row0).astype(jnp.float32)
    north_ok = jnp.where(north_n > g_n, 1.0, 0.0)
    south_ok = jnp.where(south_n > total_rows - 1 - g_n, 1.0, 0.0)
    need_n = jnp.where(behind_n, 1.0, 0.0)
    need_s = jnp.where(behind_s, 1.0, 0.0)
    near = (jnp.abs(r_key - r_n) <= RADIUS) & (jnp.abs(c_key - c_n) <= RADIUS)
    ok = jnp.where(near, 1.0, 0.0) * valid
    ok = jnp.where(need_n > north_ok, 0.0, ok)
    ok = jnp.where(need_s > south_ok, 0.0, ok)
    bias = jnp.where(ok > 0.5, 0.0, NEG)
    count = near_ref.shape[1]
    near_ref[...] = bias[:, 0:count]
    far_ref[...] = bias[:, count:]
    out_t_ref[...] = bias.T


def assemble(target, *pieces):
    at = 0
    for piece in pieces:
        target[at : at + piece.shape[0]] = piece[...]
        at += piece.shape[0]


NT = (((1,), (1,)), ((), ()))
SCALE = 1.0 / math.sqrt(HEAD_DIM)


def lanes_of(shape, j):
    lane = lax.broadcasted_iota(jnp.int32, shape, 1)
    return (lane >= j * HEAD_DIM) & (lane < (j + 1) * HEAD_DIM)


def spread(x):
    per = LANES // HEAD_DIM
    return jnp.concatenate(
        [jnp.where(lanes_of(x.shape, j), x, jnp.zeros_like(x)) for j in range(per)], axis=0
    )


def gather(x):
    per = LANES // HEAD_DIM
    count = x.shape[0] // per
    total = x[0:count]
    for j in range(1, per):
        total = jnp.where(lanes_of((count, LANES), j), x[j * count : (j + 1) * count], total)
    return total


def part(x, j, axis):
    count = x.shape[axis] // (LANES // HEAD_DIM)
    return lax.slice_in_dim(x, j * count, (j + 1) * count, axis=axis)


def groups(width):
    for g in range(width // LANES):
        yield slice(g * LANES, (g + 1) * LANES), g * (LANES // HEAD_DIM)


def dot_nt(a, b):
    return lax.dot_general(a, b, NT, preferred_element_type=jnp.float32)


def partial_stats(q_ref, g_ref, keys, values, bias, top_ref, sum_ref, dot_ref):
    for at, first in groups(q_ref.shape[1]):
        s_all = dot_nt(keys[:, at], spread(q_ref[:, at]))
        gp_all = dot_nt(values[:, at], spread(g_ref[:, at]))
        for j in range(LANES // HEAD_DIM):
            s, gp = part(s_all, j, 1) * (SCALE * LOG2E) + bias, part(gp_all, j, 1)
            top = jnp.max(s, axis=0, keepdims=True)
            e = jnp.exp2(s - top)
            h = first + j
            top_ref[h : h + 1, :] = top
            sum_ref[h : h + 1, :] = jnp.sum(e, axis=0, keepdims=True)
            dot_ref[h : h + 1, :] = jnp.sum(e * gp, axis=0, keepdims=True)


def near_stats_kernel(
    q_ref, g_ref, k_ref, v_ref, k_oth, v_oth, lc_ref, s2_ref, bias_ref,
    kall_ref, vall_ref, top_ref, sum_ref, dot_ref,
):
    assemble(kall_ref, k_ref, k_oth, lc_ref.at[0], s2_ref.at[0])
    assemble(vall_ref, v_ref, v_oth, lc_ref.at[1], s2_ref.at[1])
    near = kall_ref.shape[0]
    partial_stats(
        q_ref, g_ref, kall_ref, vall_ref, bias_ref[0:near, :], top_ref, sum_ref, dot_ref
    )


def far_stats_kernel(
    q_ref, g_ref, off_ref, corner_ref, bias_ref, top_ref, sum_ref, dot_ref,
    st_ref, kall_ref, vall_ref, top2, sum2, dot2,
):
    assemble(kall_ref, off_ref.at[0], corner_ref.at[0])
    assemble(vall_ref, off_ref.at[1], corner_ref.at[1])
    near = bias_ref.shape[0] - kall_ref.shape[0]
    partial_stats(q_ref, g_ref, kall_ref, vall_ref, bias_ref[near:, :], top2, sum2, dot2)
    top = jnp.maximum(top_ref[...], top2[...])
    a, b = jnp.exp2(top_ref[...] - top), jnp.exp2(top2[...] - top)
    total = sum_ref[...] * a + sum2[...] * b
    log_total = top + jnp.log2(total)
    dot = (dot_ref[...] * a + dot2[...] * b) / total
    terms = []
    for x in (log_total, dot):
        high = x.astype(jnp.bfloat16).astype(jnp.float32)
        mid = (x - high).astype(jnp.bfloat16).astype(jnp.float32)
        terms += [high, mid, x - high - mid]
    count = sum(x.shape[0] for x in terms)
    terms.append(jnp.zeros((LANES - count, top.shape[1]), jnp.float32))
    st_ref[...] = jnp.concatenate(terms, axis=0).T.astype(jnp.bfloat16)


def first_lanes(width):
    return width // LANES * 3 // 4 * LANES


def query_kernel(
    q_ref, g_ref, k_near, v_near, k_far, v_far, bias_near, bias_far, st_ref, *refs
):
    dq_ref = refs[-1]
    split = first_lanes(q_ref.shape[1])
    if len(refs) > 1:
        dq_ref[:, 0:split] = refs[0][...]
    heads = q_ref.shape[1] // HEAD_DIM
    per = LANES // HEAD_DIM
    row = lax.broadcasted_iota(jnp.int32, (LANES, LANES), 0)
    sides = ((k_near, v_near, bias_near), (k_far, v_far, bias_far))

    def stat_of(h):
        choose = (row == h) | (row == h + heads) | (row == h + 2 * heads)
        choose = jnp.where(choose, 1.0, 0.0).astype(jnp.bfloat16)
        return jnp.dot(st_ref[...], choose, preferred_element_type=jnp.float32)

    def wide(x, count):
        return jnp.concatenate([x] * -(-count // LANES), axis=1)[:, :count]

    for at, first in groups(q_ref.shape[1]):
        if (at.start >= split) != (len(refs) > 1):
            continue
        qs, gs = spread(q_ref[:, at]), spread(g_ref[:, at])
        logs = [stat_of(first + j) for j in range(per)]
        dots = [stat_of(first + j + 3 * heads) for j in range(per)]
        total = jnp.zeros((q_ref.shape[0], LANES), jnp.float32)
        for keys, values, bias in sides:
            kg, vg = keys[:, at], values[:, at]
            count = kg.shape[0]
            s, gp = dot_nt(qs, kg), dot_nt(gs, vg)
            ds = []
            for j in range(per):
                p = jnp.exp2(part(s, j, 0) * (SCALE * LOG2E) + (bias[...] - wide(logs[j], count)))
                ds.append((p * (part(gp, j, 0) - wide(dots[j], count))).astype(jnp.bfloat16))
            ds = jnp.concatenate(ds, axis=0)
            total += gather(jnp.dot(ds, kg, preferred_element_type=jnp.float32))
        dq_ref[:, at] = (total * SCALE).astype(jnp.bfloat16)


def key_sums(k_ref, v_ref, queries, grads, stats, bias, stat_rows, finish):
    heads = k_ref.shape[1] // HEAD_DIM
    row = lax.broadcasted_iota(jnp.int32, (2 * heads, LANES), 0)
    col = lax.broadcasted_iota(jnp.int32, (2 * heads, LANES), 1)
    base = jnp.where(row < heads, row, row + 2 * heads)
    choose = (col == base) | (col == base + heads) | (col == base + 2 * heads)
    choose = jnp.where(choose, 1.0, 0.0).astype(jnp.bfloat16)
    stat_rows[...] = dot_nt(choose, stats[...])
    for at, first in groups(k_ref.shape[1]):
        qg, gg = queries[:, at], grads[:, at]
        s, gp = dot_nt(spread(k_ref[:, at]), qg), dot_nt(spread(v_ref[:, at]), gg)
        p_half, ds = [], []
        for j in range(LANES // HEAD_DIM):
            h = first + j
            log_total, dot = stat_rows[h : h + 1, :], stat_rows[h + heads : h + heads + 1, :]
            p = jnp.exp2(part(s, j, 0) * (SCALE * LOG2E) + (bias - log_total))
            p_half.append(p.astype(jnp.bfloat16))
            ds.append((p * (part(gp, j, 0) - dot)).astype(jnp.bfloat16))
        dv = jnp.dot(jnp.concatenate(p_half, axis=0), gg, preferred_element_type=jnp.float32)
        dk = jnp.dot(jnp.concatenate(ds, axis=0), qg, preferred_element_type=jnp.float32)
        finish(at, gather(dk), gather(dv))


def near_key_kernel(
    k_ref, v_ref, q_ref, g_ref, q_oth, g_oth, lc_ref, s2_ref,
    st_ref, st_oth, st_lc, st_s2, bias_ref, dk_ref, dv_ref, qall, gall, stall, stat_rows,
):
    assemble(qall, q_ref, q_oth, lc_ref.at[0], s2_ref.at[0])
    assemble(gall, g_ref, g_oth, lc_ref.at[1], s2_ref.at[1])
    assemble(stall, st_ref, st_oth, st_lc, st_s2)

    def finish(at, dk, dv):
        dk_ref[:, at], dv_ref[:, at] = dk, dv

    key_sums(k_ref, v_ref, qall, gall, stall, bias_ref[...], stat_rows, finish)


def far_key_kernel(
    k_ref, v_ref, off_ref, st_off, bias_ref, dk_in, dv_in, dk_ref, dv_ref, stat_rows
):

    def finish(at, dk, dv):
        dk_ref[:, at] = ((dk_in[:, at] + dk) * SCALE).astype(jnp.bfloat16)
        dv_ref[:, at] = (dv_in[:, at] + dv).astype(jnp.bfloat16)

    key_sums(k_ref, v_ref, off_ref.at[0], off_ref.at[1], st_off, bias_ref[...], stat_rows, finish)


def shards(lat_count, lon_count, query, key, value, grad, pole_reach):
    rows, cols, width = query.shape
    lat, lon = lax.axis_index("lat"), lax.axis_index("lon")
    odd = lax.rem(lat, 2)
    even = odd == 0
    pair, around, across = routes(lat_count, lon_count)
    axes = ("lat", "lon")
    n_own, n_oth, n_strip, _, n_off, n_corner = pieces(rows, cols)
    near = n_own + n_oth + 2 * n_strip
    far = n_off + n_corner
    place = jnp.stack([lat, lon]).astype(jnp.int32)

    smem = pl.BlockSpec(memory_space=pltpu.SMEM)
    vmem = pl.BlockSpec(memory_space=pltpu.VMEM)

    def call(body, outs, operands, scratch=(), flops=1 << 10, scalars=False, space=pltpu.VMEM):
        return pl.pallas_call(
            body,
            out_shape=outs,
            in_specs=[smem] * scalars
            + [pl.BlockSpec(memory_space=space)] * (len(operands) - scalars),
            out_specs=jax.tree.map(lambda _: vmem, outs),
            scratch_shapes=scratch,
            compiler_params=pltpu.CompilerParams(vmem_limit_bytes=16 << 20),
            cost_estimate=pl.CostEstimate(flops=flops, bytes_accessed=1 << 10, transcendentals=0),
        )(*operands)

    def array(*shape, dtype=jnp.bfloat16):
        return jax.ShapeDtypeStruct(shape, dtype)

    f32 = jnp.float32
    heads = width // HEAD_DIM

    def strip_of(mine, other):
        side = [jnp.where(even, x[:, cols - RADIUS :], x[:, :RADIUS]) for x in (mine, other)]
        return jnp.concatenate([x.reshape(rows * RADIUS, -1) for x in side], axis=0)

    def edge_of(mine):
        return jnp.where(even, mine[:RADIUS], mine[rows - RADIUS :]).reshape(n_off, -1)

    def corner_of(first, second):
        count, half = RADIUS * RADIUS, n_strip // 2
        parts = [
            jnp.where(even, x[at : at + count], x[at + half - count : at + half])
            for x, at in ((first, 0), (second, half))
        ]
        parts.append(jnp.zeros((n_corner - 2 * count, first.shape[1]), first.dtype))
        return jnp.concatenate(parts, axis=0)

    def send(block, route):
        return lax.ppermute(block, axes, route)

    def flat(field):
        return field.reshape(n_own, field.shape[-1])

    def strips(mine, other):
        return jnp.stack([strip_of(a, b) for a, b in zip(mine, other)])

    def edges(mine):
        return jnp.stack([edge_of(a) for a in mine])

    def corners(first, second):
        return jnp.stack([corner_of(a, b) for a, b in zip(first, second)])

    key_o, value_o = send(key, pair), send(value, pair)
    query_o, grad_o = send(query, pair), send(grad, pair)
    mine = lax.optimization_barrier(jnp.stack([key, value, query, grad]))
    kv_strip = strips(mine[:2], (key_o, value_o))
    later, _ = lax.optimization_barrier((mine, kv_strip))
    kv_edge = edges(later[:2])
    kv_1 = send(kv_strip, around)
    kv_off = send(kv_edge, across)
    qg_1 = send(strips(later[2:], (query_o, grad_o)), around)
    kv_2 = send(kv_1, pair)
    kv_last = corners(kv_1, kv_2)
    kv_corner = send(kv_last, across)
    place, pole_reach, _ = lax.optimization_barrier((place, pole_reach, kv_1))
    table = np.concatenate(
        [layout(rows, cols, odd, pole) for odd in (False, True) for pole in (False, True)]
    )
    bias_near, bias_far, bias_t = call(
        functools.partial(mask_kernel, rows, cols, lat_count, lon_count),
        (
            array(n_own, near, dtype=f32),
            array(n_own, far, dtype=f32),
            array(near + far, n_own, dtype=f32),
        ),
        (place, pole_reach, jnp.asarray(table)),
        [
            pltpu.VMEM(pole_reach.shape, jnp.int32),
            pltpu.VMEM(table.shape, jnp.int32),
            pltpu.SemaphoreType.DMA((2,)),
        ],
        scalars=True,
        space=pltpu.HBM,
    )

    k, v, q, g = (flat(x) for x in mine)
    stat = array(heads, n_own, dtype=f32)
    k_near, v_near, *near_stats = call(
        near_stats_kernel,
        (array(near, width), array(near, width), stat, stat, stat),
        (q, g, k, v, flat(key_o), flat(value_o), kv_1, kv_2, bias_t),
    )
    qg_1, _ = lax.optimization_barrier((qg_1, near_stats[0]))
    qg_2 = send(qg_1, pair)
    qg_beyond = jnp.concatenate([edges(later[2:]), corners(qg_1, qg_2)], axis=1)
    near_stats[0], qg_2 = lax.optimization_barrier((near_stats[0], qg_2))
    stats, k_far, v_far = call(
        far_stats_kernel,
        (array(n_own, LANES), array(far, width), array(far, width)),
        (q, g, kv_off, kv_corner, bias_t, *near_stats),
        [pltpu.VMEM((heads, n_own), f32)] * 3,
    )
    stats_grid = stats.reshape(rows, cols, LANES)
    stats_o = send(stats_grid, pair)
    st_strip, stats_q = lax.optimization_barrier((strip_of(stats_grid, stats_o), stats))
    st_1 = send(st_strip, around)
    qg_off = send(qg_beyond, across)
    query_side = (q, g, k_near, v_near, k_far, v_far, bias_near, bias_far)
    d_query = call(query_kernel, array(n_own, first_lanes(width)), (*query_side, stats_q))
    st_1, d_query = lax.optimization_barrier((st_1, d_query))
    st_2 = send(st_1, pair)
    _, stats_q = lax.optimization_barrier((st_2, stats))
    st_off = send(
        jnp.concatenate([edge_of(stats_grid), corner_of(st_1, st_2)], axis=0), across
    )

    d_query = call(query_kernel, array(n_own, width), (*query_side, stats_q, d_query))
    d_key, d_value = call(
        near_key_kernel,
        (array(n_own, width, dtype=f32),) * 2,
        (
            k, v, q, g, flat(query_o), flat(grad_o), qg_1, qg_2,
            stats, flat(stats_o), st_1, st_2, bias_near,
        ),
        [
            pltpu.VMEM((near, width), jnp.bfloat16),
            pltpu.VMEM((near, width), jnp.bfloat16),
            pltpu.VMEM((near, LANES), jnp.bfloat16),
            pltpu.VMEM((2 * heads, near), f32),
        ],
    )
    d_key, d_value = call(
        far_key_kernel,
        (array(n_own, width), array(n_own, width)),
        (k, v, qg_off, st_off, bias_far, d_key, d_value),
        [pltpu.VMEM((2 * heads, far), f32)],
    )
    shape = (rows, cols, width)
    return d_query.reshape(shape), d_key.reshape(shape), d_value.reshape(shape)


def solution(mesh):
    field = P("lat", "lon", None)
    return jax.shard_map(
        functools.partial(shards, mesh.shape["lat"], mesh.shape["lon"]),
        mesh=mesh,
        in_specs=(field, field, field, field, P()),
        out_specs=(field, field, field),
        check_vma=False,
    )
```

```python
import functools
import math

import jax
import jax.numpy as jnp
import numpy as np
from jax import lax
from jax.experimental import pallas as pl
from jax.experimental.pallas import tpu as pltpu
from jax.sharding import PartitionSpec as P

HEAD_DIM = 32
RADIUS = 6
LANES = 128
NEG = -1e30
LOG2E = 1.4426950408889634


def routes(lat_count, lon_count):
    half = lon_count // 2
    pair, around, across = [], [], []
    for i in range(lat_count):
        for j in range(lon_count):
            me = i * lon_count + j
            pair.append((me, (i ^ 1) * lon_count + j))
            step = 1 if i % 2 == 0 else -1
            around.append((me, i * lon_count + (j + step) % lon_count))
            other = i - 1 if i % 2 == 0 else i + 1
            if 0 <= other < lat_count:
                across.append((me, other * lon_count + j))
            else:
                across.append((me, i * lon_count + (j + half) % lon_count))
    return pair, around, across


def pieces(rows, cols):
    corners = 2 * RADIUS * RADIUS
    pad = -corners % 8
    strip = 2 * rows * RADIUS
    return rows * cols, rows * cols, strip, strip, RADIUS * cols, corners + pad


def layout(rows, cols, odd, pole):
    west, east = range(-RADIUS, 0), range(cols, cols + RADIUS)
    mine, other = range(0, rows), range(-rows, 0) if odd else range(rows, 2 * rows)
    beyond = range(rows, rows + RADIUS) if odd else range(-RADIUS, 0)
    if pole:
        beyond = beyond[::-1]
    sender_odd = odd if pole else not odd
    places = [(r, c) for r in range(rows) for c in range(cols)]
    places += [(r + (-rows if odd else rows), c) for r, c in places]
    first, second = (east, west) if odd else (west, east)
    for side, bands in ((first, (mine, other)), (second, (other, mine))):
        places += [(r, c) for band in bands for r in band for c in side]
    places += [(r, c) for r in beyond for c in range(cols)]
    for side in (east, west) if sender_odd else (west, east):
        places += [(r, c) for r in beyond for c in side]
    nowhere = (1 << 20, 0)
    places += [nowhere] * (sum(pieces(rows, cols)) - len(places))
    return np.array(places, np.int32).T


def mask_kernel(
    rows, cols, lat_count, lon_count, sc_ref, reach_hbm, table_hbm,
    near_ref, far_ref, out_t_ref, reach_vm, table_ref, sems,
):
    copies = [
        pltpu.make_async_copy(reach_hbm, reach_vm, sems.at[0]),
        pltpu.make_async_copy(table_hbm, table_ref, sems.at[1]),
    ]
    for copy in copies:
        copy.start()
    for copy in copies:
        copy.wait()
    reach = reach_vm[...].astype(jnp.float32)
    lat, lon = sc_ref[0], sc_ref[1]
    total_rows, total_cols = rows * lat_count, cols * lon_count
    odd = lax.rem(lat, 2)
    pole = jnp.where(jnp.where(odd == 0, lat, lat_count - 1 - lat) == 0, 1, 0)
    row0, col0 = lat * rows, lon * cols
    which = 2 * (2 * odd + pole)
    r_key = table_ref[pl.ds(which, 1), :]
    c_key = table_ref[pl.ds(which + 1, 1), :]
    outer = r_key.shape[1]
    g_key = r_key + row0
    turned = lax.rem(c_key + (col0 + total_cols // 2 + total_cols), total_cols)
    pick = lax.broadcasted_iota(jnp.int32, (total_cols, outer), 0) == turned
    pick = jnp.where(pick, 1.0, 0.0)
    key_reach = jnp.dot(reach, pick, preferred_element_type=jnp.float32)
    north_key, south_key = key_reach[0:1], key_reach[1:2]
    g_f = g_key.astype(jnp.float32)
    behind_n = g_key < 0
    behind_s = g_key >= total_rows
    spare = jnp.where(
        behind_n, north_key + 1.0 + g_f, jnp.where(behind_s, south_key + total_rows - g_f, 1.0)
    )
    valid = jnp.where(spare > 0.5, 1.0, 0.0)
    n = lax.broadcasted_iota(jnp.int32, (rows * cols, 1), 0)
    shift = cols.bit_length() - 1
    r_n, c_n = lax.shift_right_logical(n, shift), n & (cols - 1)
    pick_n = lax.broadcasted_iota(jnp.int32, (rows * cols, total_cols), 1) == (c_n + col0)
    north_n = jnp.sum(jnp.where(pick_n, reach[0:1, :], 0.0), axis=1, keepdims=True)
    south_n = jnp.sum(jnp.where(pick_n, reach[1:2, :], 0.0), axis=1, keepdims=True)
    g_n = (r_n + row0).astype(jnp.float32)
    north_ok = jnp.where(north_n > g_n, 1.0, 0.0)
    south_ok = jnp.where(south_n > total_rows - 1 - g_n, 1.0, 0.0)
    need_n = jnp.where(behind_n, 1.0, 0.0)
    need_s = jnp.where(behind_s, 1.0, 0.0)
    near = (jnp.abs(r_key - r_n) <= RADIUS) & (jnp.abs(c_key - c_n) <= RADIUS)
    ok = jnp.where(near, 1.0, 0.0) * valid
    ok = jnp.where(need_n > north_ok, 0.0, ok)
    ok = jnp.where(need_s > south_ok, 0.0, ok)
    bias = jnp.where(ok > 0.5, 0.0, NEG)
    count = near_ref.shape[1]
    near_ref[...] = bias[:, 0:count]
    far_ref[...] = bias[:, count:]
    out_t_ref[...] = bias.T


def assemble(target, *pieces):
    at = 0
    for piece in pieces:
        target[at : at + piece.shape[0]] = piece[...]
        at += piece.shape[0]


NT = (((1,), (1,)), ((), ()))
SCALE = 1.0 / math.sqrt(HEAD_DIM)


def lanes_of(shape, j):
    lane = lax.broadcasted_iota(jnp.int32, shape, 1)
    return (lane >= j * HEAD_DIM) & (lane < (j + 1) * HEAD_DIM)


def spread(x):
    per = LANES // HEAD_DIM
    return jnp.concatenate(
        [jnp.where(lanes_of(x.shape, j), x, jnp.zeros_like(x)) for j in range(per)], axis=0
    )


def gather(x):
    per = LANES // HEAD_DIM
    count = x.shape[0] // per
    total = x[0:count]
    for j in range(1, per):
        total = jnp.where(lanes_of((count, LANES), j), x[j * count : (j + 1) * count], total)
    return total


def part(x, j, axis):
    count = x.shape[axis] // (LANES // HEAD_DIM)
    return lax.slice_in_dim(x, j * count, (j + 1) * count, axis=axis)


def groups(width):
    for g in range(width // LANES):
        yield slice(g * LANES, (g + 1) * LANES), g * (LANES // HEAD_DIM)


def dot_nt(a, b):
    return lax.dot_general(a, b, NT, preferred_element_type=jnp.float32)


def partial_stats(q_ref, g_ref, keys, values, bias, top_ref, sum_ref, dot_ref):
    for at, first in groups(q_ref.shape[1]):
        s_all = dot_nt(keys[:, at], spread(q_ref[:, at]))
        gp_all = dot_nt(values[:, at], spread(g_ref[:, at]))
        for j in range(LANES // HEAD_DIM):
            s, gp = part(s_all, j, 1) * (SCALE * LOG2E) + bias, part(gp_all, j, 1)
            top = jnp.max(s, axis=0, keepdims=True)
            e = jnp.exp2(s - top)
            h = first + j
            top_ref[h : h + 1, :] = top
            sum_ref[h : h + 1, :] = jnp.sum(e, axis=0, keepdims=True)
            dot_ref[h : h + 1, :] = jnp.sum(e * gp, axis=0, keepdims=True)


def near_stats_kernel(
    q_ref, g_ref, k_ref, v_ref, k_oth, v_oth, lc_ref, s2_ref, bias_ref,
    kall_ref, vall_ref, top_ref, sum_ref, dot_ref,
):
    assemble(kall_ref, k_ref, k_oth, lc_ref.at[0], s2_ref.at[0])
    assemble(vall_ref, v_ref, v_oth, lc_ref.at[1], s2_ref.at[1])
    near = kall_ref.shape[0]
    partial_stats(
        q_ref, g_ref, kall_ref, vall_ref, bias_ref[0:near, :], top_ref, sum_ref, dot_ref
    )


def far_stats_kernel(
    q_ref, g_ref, off_ref, corner_ref, bias_ref, top_ref, sum_ref, dot_ref,
    st_ref, kall_ref, vall_ref, top2, sum2, dot2,
):
    assemble(kall_ref, off_ref.at[0], corner_ref.at[0])
    assemble(vall_ref, off_ref.at[1], corner_ref.at[1])
    near = bias_ref.shape[0] - kall_ref.shape[0]
    partial_stats(q_ref, g_ref, kall_ref, vall_ref, bias_ref[near:, :], top2, sum2, dot2)
    top = jnp.maximum(top_ref[...], top2[...])
    a, b = jnp.exp2(top_ref[...] - top), jnp.exp2(top2[...] - top)
    total = sum_ref[...] * a + sum2[...] * b
    log_total = top + jnp.log2(total)
    dot = (dot_ref[...] * a + dot2[...] * b) / total
    terms = []
    for x in (log_total, dot):
        high = x.astype(jnp.bfloat16).astype(jnp.float32)
        mid = (x - high).astype(jnp.bfloat16).astype(jnp.float32)
        terms += [high, mid, x - high - mid]
    count = sum(x.shape[0] for x in terms)
    terms.append(jnp.zeros((LANES - count, top.shape[1]), jnp.float32))
    st_ref[...] = jnp.concatenate(terms, axis=0).T.astype(jnp.bfloat16)


def first_lanes(width):
    return width // LANES * 3 // 4 * LANES


def query_kernel(
    q_ref, g_ref, k_near, v_near, k_far, v_far, bias_near, bias_far, st_ref, *refs
):
    dq_ref = refs[-1]
    split = first_lanes(q_ref.shape[1])
    if len(refs) > 1:
        dq_ref[:, 0:split] = refs[0][...]
    heads = q_ref.shape[1] // HEAD_DIM
    per = LANES // HEAD_DIM
    row = lax.broadcasted_iota(jnp.int32, (LANES, LANES), 0)
    sides = ((k_near, v_near, bias_near), (k_far, v_far, bias_far))

    def stat_of(h):
        choose = (row == h) | (row == h + heads) | (row == h + 2 * heads)
        choose = jnp.where(choose, 1.0, 0.0).astype(jnp.bfloat16)
        return jnp.dot(st_ref[...], choose, preferred_element_type=jnp.float32)

    def wide(x, count):
        return jnp.concatenate([x] * -(-count // LANES), axis=1)[:, :count]

    for at, first in groups(q_ref.shape[1]):
        if (at.start >= split) != (len(refs) > 1):
            continue
        qs, gs = spread(q_ref[:, at]), spread(g_ref[:, at])
        logs = [stat_of(first + j) for j in range(per)]
        dots = [stat_of(first + j + 3 * heads) for j in range(per)]
        total = jnp.zeros((q_ref.shape[0], LANES), jnp.float32)
        for keys, values, bias in sides:
            kg, vg = keys[:, at], values[:, at]
            count = kg.shape[0]
            s, gp = dot_nt(qs, kg), dot_nt(gs, vg)
            ds = []
            for j in range(per):
                p = jnp.exp2(part(s, j, 0) * (SCALE * LOG2E) + (bias[...] - wide(logs[j], count)))
                ds.append((p * (part(gp, j, 0) - wide(dots[j], count))).astype(jnp.bfloat16))
            ds = jnp.concatenate(ds, axis=0)
            total += gather(jnp.dot(ds, kg, preferred_element_type=jnp.float32))
        dq_ref[:, at] = (total * SCALE).astype(jnp.bfloat16)


def key_sums(k_ref, v_ref, queries, grads, stats, bias, stat_rows, finish):
    heads = k_ref.shape[1] // HEAD_DIM
    row = lax.broadcasted_iota(jnp.int32, (2 * heads, LANES), 0)
    col = lax.broadcasted_iota(jnp.int32, (2 * heads, LANES), 1)
    base = jnp.where(row < heads, row, row + 2 * heads)
    choose = (col == base) | (col == base + heads) | (col == base + 2 * heads)
    choose = jnp.where(choose, 1.0, 0.0).astype(jnp.bfloat16)
    stat_rows[...] = dot_nt(choose, stats[...])
    for at, first in groups(k_ref.shape[1]):
        qg, gg = queries[:, at], grads[:, at]
        s, gp = dot_nt(spread(k_ref[:, at]), qg), dot_nt(spread(v_ref[:, at]), gg)
        p_half, ds = [], []
        for j in range(LANES // HEAD_DIM):
            h = first + j
            log_total, dot = stat_rows[h : h + 1, :], stat_rows[h + heads : h + heads + 1, :]
            p = jnp.exp2(part(s, j, 0) * (SCALE * LOG2E) + (bias - log_total))
            p_half.append(p.astype(jnp.bfloat16))
            ds.append((p * (part(gp, j, 0) - dot)).astype(jnp.bfloat16))
        dv = jnp.dot(jnp.concatenate(p_half, axis=0), gg, preferred_element_type=jnp.float32)
        dk = jnp.dot(jnp.concatenate(ds, axis=0), qg, preferred_element_type=jnp.float32)
        finish(at, gather(dk), gather(dv))


def near_key_kernel(
    k_ref, v_ref, q_ref, g_ref, q_oth, g_oth, lc_ref, s2_ref,
    st_ref, st_oth, st_lc, st_s2, bias_ref, dk_ref, dv_ref, qall, gall, stall, stat_rows,
):
    assemble(qall, q_ref, q_oth, lc_ref.at[0], s2_ref.at[0])
    assemble(gall, g_ref, g_oth, lc_ref.at[1], s2_ref.at[1])
    assemble(stall, st_ref, st_oth, st_lc, st_s2)

    def finish(at, dk, dv):
        dk_ref[:, at], dv_ref[:, at] = dk, dv

    key_sums(k_ref, v_ref, qall, gall, stall, bias_ref[...], stat_rows, finish)


def second_leg_kernel(count, *refs):
    outs = len(refs) - 4 - 3
    near_key_kernel(*refs[count:outs], *refs[outs + 1 :])
    query_kernel(*refs[:count], refs[outs])


def far_key_kernel(
    k_ref, v_ref, off_ref, st_off, bias_ref, dk_in, dv_in, dk_ref, dv_ref, stat_rows
):

    def finish(at, dk, dv):
        dk_ref[:, at] = ((dk_in[:, at] + dk) * SCALE).astype(jnp.bfloat16)
        dv_ref[:, at] = (dv_in[:, at] + dv).astype(jnp.bfloat16)

    key_sums(k_ref, v_ref, off_ref.at[0], off_ref.at[1], st_off, bias_ref[...], stat_rows, finish)


def shards(lat_count, lon_count, query, key, value, grad, pole_reach):
    rows, cols, width = query.shape
    lat, lon = lax.axis_index("lat"), lax.axis_index("lon")
    odd = lax.rem(lat, 2)
    even = odd == 0
    pair, around, across = routes(lat_count, lon_count)
    axes = ("lat", "lon")
    n_own, n_oth, n_strip, _, n_off, n_corner = pieces(rows, cols)
    near = n_own + n_oth + 2 * n_strip
    far = n_off + n_corner
    place = jnp.stack([lat, lon]).astype(jnp.int32)

    smem = pl.BlockSpec(memory_space=pltpu.SMEM)
    vmem = pl.BlockSpec(memory_space=pltpu.VMEM)

    def call(body, outs, operands, scratch=(), flops=1 << 10, scalars=False, space=pltpu.VMEM):
        return pl.pallas_call(
            body,
            out_shape=outs,
            in_specs=[smem] * scalars
            + [pl.BlockSpec(memory_space=space)] * (len(operands) - scalars),
            out_specs=jax.tree.map(lambda _: vmem, outs),
            scratch_shapes=scratch,
            compiler_params=pltpu.CompilerParams(vmem_limit_bytes=16 << 20),
            cost_estimate=pl.CostEstimate(flops=flops, bytes_accessed=1 << 10, transcendentals=0),
        )(*operands)

    def array(*shape, dtype=jnp.bfloat16):
        return jax.ShapeDtypeStruct(shape, dtype)

    f32 = jnp.float32
    heads = width // HEAD_DIM

    def strip_of(mine, other):
        side = [jnp.where(even, x[:, cols - RADIUS :], x[:, :RADIUS]) for x in (mine, other)]
        return jnp.concatenate([x.reshape(rows * RADIUS, -1) for x in side], axis=0)

    def edge_of(mine):
        return jnp.where(even, mine[:RADIUS], mine[rows - RADIUS :]).reshape(n_off, -1)

    def corner_of(first, second):
        count, half = RADIUS * RADIUS, n_strip // 2
        parts = [
            jnp.where(even, x[at : at + count], x[at + half - count : at + half])
            for x, at in ((first, 0), (second, half))
        ]
        parts.append(jnp.zeros((n_corner - 2 * count, first.shape[1]), first.dtype))
        return jnp.concatenate(parts, axis=0)

    def send(block, route):
        return lax.ppermute(block, axes, route)

    def flat(field):
        return field.reshape(n_own, field.shape[-1])

    def strips(mine, other):
        return jnp.stack([strip_of(a, b) for a, b in zip(mine, other)])

    def edges(mine):
        return jnp.stack([edge_of(a) for a in mine])

    def corners(first, second):
        return jnp.stack([corner_of(a, b) for a, b in zip(first, second)])

    key_o, value_o = send(key, pair), send(value, pair)
    query_o, grad_o = send(query, pair), send(grad, pair)
    mine = lax.optimization_barrier(jnp.stack([key, value, query, grad]))
    kv_strip = strips(mine[:2], (key_o, value_o))
    later, _ = lax.optimization_barrier((mine, kv_strip))
    kv_edge = edges(later[:2])
    kv_1 = send(kv_strip, around)
    kv_off = send(kv_edge, across)
    qg_1 = send(strips(later[2:], (query_o, grad_o)), around)
    kv_2 = send(kv_1, pair)
    kv_last = corners(kv_1, kv_2)
    kv_corner = send(kv_last, across)
    place, pole_reach, _ = lax.optimization_barrier((place, pole_reach, kv_1))
    table = np.concatenate(
        [layout(rows, cols, odd, pole) for odd in (False, True) for pole in (False, True)]
    )
    bias_near, bias_far, bias_t = call(
        functools.partial(mask_kernel, rows, cols, lat_count, lon_count),
        (
            array(n_own, near, dtype=f32),
            array(n_own, far, dtype=f32),
            array(near + far, n_own, dtype=f32),
        ),
        (place, pole_reach, jnp.asarray(table)),
        [
            pltpu.VMEM(pole_reach.shape, jnp.int32),
            pltpu.VMEM(table.shape, jnp.int32),
            pltpu.SemaphoreType.DMA((2,)),
        ],
        scalars=True,
        space=pltpu.HBM,
    )

    k, v, q, g = (flat(x) for x in mine)
    stat = array(heads, n_own, dtype=f32)
    k_near, v_near, *near_stats = call(
        near_stats_kernel,
        (array(near, width), array(near, width), stat, stat, stat),
        (q, g, k, v, flat(key_o), flat(value_o), kv_1, kv_2, bias_t),
    )
    qg_1, _ = lax.optimization_barrier((qg_1, near_stats[0]))
    qg_2 = send(qg_1, pair)
    qg_beyond = jnp.concatenate([edges(later[2:]), corners(qg_1, qg_2)], axis=1)
    near_stats[0], qg_2 = lax.optimization_barrier((near_stats[0], qg_2))
    stats, k_far, v_far = call(
        far_stats_kernel,
        (array(n_own, LANES), array(far, width), array(far, width)),
        (q, g, kv_off, kv_corner, bias_t, *near_stats),
        [pltpu.VMEM((heads, n_own), f32)] * 3,
    )
    stats_grid = stats.reshape(rows, cols, LANES)
    stats_o = send(stats_grid, pair)
    st_strip, stats_q = lax.optimization_barrier((strip_of(stats_grid, stats_o), stats))
    st_1 = send(st_strip, around)
    qg_off = send(qg_beyond, across)
    query_side = (q, g, k_near, v_near, k_far, v_far, bias_near, bias_far)
    d_query = call(query_kernel, array(n_own, first_lanes(width)), (*query_side, stats_q))
    st_1, d_query = lax.optimization_barrier((st_1, d_query))
    st_2 = send(st_1, pair)
    _, stats_q = lax.optimization_barrier((st_2, stats))
    st_off = send(
        jnp.concatenate([edge_of(stats_grid), corner_of(st_1, st_2)], axis=0), across
    )

    first_args = (*query_side, stats_q, d_query)
    d_query, d_key, d_value = call(
        functools.partial(second_leg_kernel, len(first_args)),
        (array(n_own, width), *(array(n_own, width, dtype=f32),) * 2),
        (
            *first_args,
            k, v, q, g, flat(query_o), flat(grad_o), qg_1, qg_2,
            stats, flat(stats_o), st_1, st_2, bias_near,
        ),
        [
            pltpu.VMEM((near, width), jnp.bfloat16),
            pltpu.VMEM((near, width), jnp.bfloat16),
            pltpu.VMEM((near, LANES), jnp.bfloat16),
            pltpu.VMEM((2 * heads, near), f32),
        ],
    )
    d_key, d_value = call(
        far_key_kernel,
        (array(n_own, width), array(n_own, width)),
        (k, v, qg_off, st_off, bias_far, d_key, d_value),
        [pltpu.VMEM((2 * heads, far), f32)],
    )
    shape = (rows, cols, width)
    return d_query.reshape(shape), d_key.reshape(shape), d_value.reshape(shape)


def solution(mesh):
    field = P("lat", "lon", None)
    return jax.shard_map(
        functools.partial(shards, mesh.shape["lat"], mesh.shape["lon"]),
        mesh=mesh,
        in_specs=(field, field, field, field, P()),
        out_specs=(field, field, field),
        check_vma=False,
    )
```

```python
import functools
import math

import jax
import jax.numpy as jnp
import numpy as np
from jax import lax
from jax.experimental import pallas as pl
from jax.experimental.pallas import tpu as pltpu
from jax.sharding import PartitionSpec as P

HEAD_DIM = 32
RADIUS = 6
LANES = 128
NEG = -1e30
LOG2E = 1.4426950408889634


def routes(lat_count, lon_count):
    half = lon_count // 2
    pair, around, across = [], [], []
    for i in range(lat_count):
        for j in range(lon_count):
            me = i * lon_count + j
            pair.append((me, (i ^ 1) * lon_count + j))
            step = 1 if i % 2 == 0 else -1
            around.append((me, i * lon_count + (j + step) % lon_count))
            other = i - 1 if i % 2 == 0 else i + 1
            if 0 <= other < lat_count:
                across.append((me, other * lon_count + j))
            else:
                across.append((me, i * lon_count + (j + half) % lon_count))
    return pair, around, across


def pieces(rows, cols):
    corners = 2 * RADIUS * RADIUS
    pad = -corners % 8
    strip = 2 * rows * RADIUS
    return rows * cols, rows * cols, strip, strip, RADIUS * cols, corners + pad


def layout(rows, cols, odd, pole):
    west, east = range(-RADIUS, 0), range(cols, cols + RADIUS)
    mine, other = range(0, rows), range(-rows, 0) if odd else range(rows, 2 * rows)
    beyond = range(rows, rows + RADIUS) if odd else range(-RADIUS, 0)
    if pole:
        beyond = beyond[::-1]
    sender_odd = odd if pole else not odd
    places = [(r, c) for r in range(rows) for c in range(cols)]
    places += [(r + (-rows if odd else rows), c) for r, c in places]
    first, second = (east, west) if odd else (west, east)
    for side, bands in ((first, (mine, other)), (second, (other, mine))):
        places += [(r, c) for band in bands for r in band for c in side]
    places += [(r, c) for r in beyond for c in range(cols)]
    for side in (east, west) if sender_odd else (west, east):
        places += [(r, c) for r in beyond for c in side]
    nowhere = (1 << 20, 0)
    places += [nowhere] * (sum(pieces(rows, cols)) - len(places))
    return np.array(places, np.int32).T


def mask_kernel(
    rows, cols, lat_count, lon_count, sc_ref, reach_hbm, table_hbm,
    near_ref, far_ref, out_t_ref, reach_vm, table_ref, sems,
):
    copies = [
        pltpu.make_async_copy(reach_hbm, reach_vm, sems.at[0]),
        pltpu.make_async_copy(table_hbm, table_ref, sems.at[1]),
    ]
    for copy in copies:
        copy.start()
    for copy in copies:
        copy.wait()
    reach = reach_vm[...].astype(jnp.float32)
    lat, lon = sc_ref[0], sc_ref[1]
    total_rows, total_cols = rows * lat_count, cols * lon_count
    odd = lax.rem(lat, 2)
    pole = jnp.where(jnp.where(odd == 0, lat, lat_count - 1 - lat) == 0, 1, 0)
    row0, col0 = lat * rows, lon * cols
    which = 2 * (2 * odd + pole)
    r_key = table_ref[pl.ds(which, 1), :]
    c_key = table_ref[pl.ds(which + 1, 1), :]
    outer = r_key.shape[1]
    g_key = r_key + row0
    turned = lax.rem(c_key + (col0 + total_cols // 2 + total_cols), total_cols)
    pick = lax.broadcasted_iota(jnp.int32, (total_cols, outer), 0) == turned
    pick = jnp.where(pick, 1.0, 0.0)
    key_reach = jnp.dot(reach, pick, preferred_element_type=jnp.float32)
    north_key, south_key = key_reach[0:1], key_reach[1:2]
    g_f = g_key.astype(jnp.float32)
    behind_n = g_key < 0
    behind_s = g_key >= total_rows
    spare = jnp.where(
        behind_n, north_key + 1.0 + g_f, jnp.where(behind_s, south_key + total_rows - g_f, 1.0)
    )
    valid = jnp.where(spare > 0.5, 1.0, 0.0)
    n = lax.broadcasted_iota(jnp.int32, (rows * cols, 1), 0)
    shift = cols.bit_length() - 1
    r_n, c_n = lax.shift_right_logical(n, shift), n & (cols - 1)
    pick_n = lax.broadcasted_iota(jnp.int32, (rows * cols, total_cols), 1) == (c_n + col0)
    north_n = jnp.sum(jnp.where(pick_n, reach[0:1, :], 0.0), axis=1, keepdims=True)
    south_n = jnp.sum(jnp.where(pick_n, reach[1:2, :], 0.0), axis=1, keepdims=True)
    g_n = (r_n + row0).astype(jnp.float32)
    north_ok = jnp.where(north_n > g_n, 1.0, 0.0)
    south_ok = jnp.where(south_n > total_rows - 1 - g_n, 1.0, 0.0)
    need_n = jnp.where(behind_n, 1.0, 0.0)
    need_s = jnp.where(behind_s, 1.0, 0.0)
    near = (jnp.abs(r_key - r_n) <= RADIUS) & (jnp.abs(c_key - c_n) <= RADIUS)
    ok = jnp.where(near, 1.0, 0.0) * valid
    ok = jnp.where(need_n > north_ok, 0.0, ok)
    ok = jnp.where(need_s > south_ok, 0.0, ok)
    bias = jnp.where(ok > 0.5, 0.0, NEG)
    count = near_ref.shape[1]
    near_ref[...] = bias[:, 0:count]
    far_ref[...] = bias[:, count:]
    out_t_ref[...] = bias.T


def assemble(target, *pieces):
    at = 0
    for piece in pieces:
        target[at : at + piece.shape[0]] = piece[...]
        at += piece.shape[0]


NT = (((1,), (1,)), ((), ()))
SCALE = 1.0 / math.sqrt(HEAD_DIM)


def lanes_of(shape, j):
    lane = lax.broadcasted_iota(jnp.int32, shape, 1)
    return (lane >= j * HEAD_DIM) & (lane < (j + 1) * HEAD_DIM)


def spread(x):
    per = LANES // HEAD_DIM
    return jnp.concatenate(
        [jnp.where(lanes_of(x.shape, j), x, jnp.zeros_like(x)) for j in range(per)], axis=0
    )


def gather(x):
    per = LANES // HEAD_DIM
    count = x.shape[0] // per
    total = x[0:count]
    for j in range(1, per):
        total = jnp.where(lanes_of((count, LANES), j), x[j * count : (j + 1) * count], total)
    return total


def part(x, j, axis):
    count = x.shape[axis] // (LANES // HEAD_DIM)
    return lax.slice_in_dim(x, j * count, (j + 1) * count, axis=axis)


def groups(width):
    for g in range(width // LANES):
        yield slice(g * LANES, (g + 1) * LANES), g * (LANES // HEAD_DIM)


def dot_nt(a, b):
    return lax.dot_general(a, b, NT, preferred_element_type=jnp.float32)


def partial_stats(q_ref, g_ref, keys, values, bias, top_ref, sum_ref, dot_ref):
    for at, first in groups(q_ref.shape[1]):
        s_all = dot_nt(keys[:, at], spread(q_ref[:, at]))
        gp_all = dot_nt(values[:, at], spread(g_ref[:, at]))
        for j in range(LANES // HEAD_DIM):
            s, gp = part(s_all, j, 1) * (SCALE * LOG2E) + bias, part(gp_all, j, 1)
            top = jnp.max(s, axis=0, keepdims=True)
            e = jnp.exp2(s - top)
            h = first + j
            top_ref[h : h + 1, :] = top
            sum_ref[h : h + 1, :] = jnp.sum(e, axis=0, keepdims=True)
            dot_ref[h : h + 1, :] = jnp.sum(e * gp, axis=0, keepdims=True)


def near_stats_kernel(
    q_ref, g_ref, k_ref, v_ref, k_oth, v_oth, lc_ref, s2_ref, bias_ref,
    kall_ref, vall_ref, top_ref, sum_ref, dot_ref,
):
    assemble(kall_ref, k_ref, k_oth, lc_ref.at[0], s2_ref.at[0])
    assemble(vall_ref, v_ref, v_oth, lc_ref.at[1], s2_ref.at[1])
    near = kall_ref.shape[0]
    partial_stats(
        q_ref, g_ref, kall_ref, vall_ref, bias_ref[0:near, :], top_ref, sum_ref, dot_ref
    )


def far_stats_kernel(
    q_ref, g_ref, off_ref, corner_ref, bias_ref, top_ref, sum_ref, dot_ref,
    st_ref, kall_ref, vall_ref, top2, sum2, dot2,
):
    assemble(kall_ref, off_ref.at[0], corner_ref.at[0])
    assemble(vall_ref, off_ref.at[1], corner_ref.at[1])
    near = bias_ref.shape[0] - kall_ref.shape[0]
    partial_stats(q_ref, g_ref, kall_ref, vall_ref, bias_ref[near:, :], top2, sum2, dot2)
    top = jnp.maximum(top_ref[...], top2[...])
    a, b = jnp.exp2(top_ref[...] - top), jnp.exp2(top2[...] - top)
    total = sum_ref[...] * a + sum2[...] * b
    log_total = top + jnp.log2(total)
    dot = (dot_ref[...] * a + dot2[...] * b) / total
    terms = []
    for x in (log_total, dot):
        high = x.astype(jnp.bfloat16).astype(jnp.float32)
        mid = (x - high).astype(jnp.bfloat16).astype(jnp.float32)
        terms += [high, mid, x - high - mid]
    count = sum(x.shape[0] for x in terms)
    terms.append(jnp.zeros((LANES - count, top.shape[1]), jnp.float32))
    st_ref[...] = jnp.concatenate(terms, axis=0).T.astype(jnp.bfloat16)


def first_lanes(width):
    return width // LANES * 3 // 4 * LANES


def query_kernel(
    q_ref, g_ref, k_near, v_near, k_far, v_far, bias_near, bias_far, st_ref, *refs
):
    dq_ref = refs[-1]
    split = first_lanes(q_ref.shape[1])
    if len(refs) > 1:
        dq_ref[:, 0:split] = refs[0][...]
    heads = q_ref.shape[1] // HEAD_DIM
    per = LANES // HEAD_DIM
    row = lax.broadcasted_iota(jnp.int32, (LANES, LANES), 0)
    sides = ((k_near, v_near, bias_near), (k_far, v_far, bias_far))

    def stat_of(h):
        choose = (row == h) | (row == h + heads) | (row == h + 2 * heads)
        choose = jnp.where(choose, 1.0, 0.0).astype(jnp.bfloat16)
        return jnp.dot(st_ref[...], choose, preferred_element_type=jnp.float32)

    def wide(x, count):
        return jnp.concatenate([x] * -(-count // LANES), axis=1)[:, :count]

    for at, first in groups(q_ref.shape[1]):
        if (at.start >= split) != (len(refs) > 1):
            continue
        qs, gs = spread(q_ref[:, at]), spread(g_ref[:, at])
        logs = [stat_of(first + j) for j in range(per)]
        dots = [stat_of(first + j + 3 * heads) for j in range(per)]
        total = jnp.zeros((q_ref.shape[0], LANES), jnp.float32)
        for keys, values, bias in sides:
            kg, vg = keys[:, at], values[:, at]
            count = kg.shape[0]
            s, gp = dot_nt(qs, kg), dot_nt(gs, vg)
            ds = []
            for j in range(per):
                p = jnp.exp2(part(s, j, 0) * (SCALE * LOG2E) + (bias[...] - wide(logs[j], count)))
                ds.append((p * (part(gp, j, 0) - wide(dots[j], count))).astype(jnp.bfloat16))
            ds = jnp.concatenate(ds, axis=0)
            total += gather(jnp.dot(ds, kg, preferred_element_type=jnp.float32))
        dq_ref[:, at] = (total * SCALE).astype(jnp.bfloat16)


def key_sums(k_ref, v_ref, queries, grads, stats, bias, stat_rows, finish):
    heads = k_ref.shape[1] // HEAD_DIM
    row = lax.broadcasted_iota(jnp.int32, (2 * heads, LANES), 0)
    col = lax.broadcasted_iota(jnp.int32, (2 * heads, LANES), 1)
    base = jnp.where(row < heads, row, row + 2 * heads)
    choose = (col == base) | (col == base + heads) | (col == base + 2 * heads)
    choose = jnp.where(choose, 1.0, 0.0).astype(jnp.bfloat16)
    stat_rows[...] = dot_nt(choose, stats[...])
    for at, first in groups(k_ref.shape[1]):
        qg, gg = queries[:, at], grads[:, at]
        s, gp = dot_nt(spread(k_ref[:, at]), qg), dot_nt(spread(v_ref[:, at]), gg)
        p_half, ds = [], []
        for j in range(LANES // HEAD_DIM):
            h = first + j
            log_total, dot = stat_rows[h : h + 1, :], stat_rows[h + heads : h + heads + 1, :]
            p = jnp.exp2(part(s, j, 0) * (SCALE * LOG2E) + (bias - log_total))
            p_half.append(p.astype(jnp.bfloat16))
            ds.append((p * (part(gp, j, 0) - dot)).astype(jnp.bfloat16))
        dv = jnp.dot(jnp.concatenate(p_half, axis=0), gg, preferred_element_type=jnp.float32)
        dk = jnp.dot(jnp.concatenate(ds, axis=0), qg, preferred_element_type=jnp.float32)
        finish(at, gather(dk), gather(dv))


def near_key_kernel(
    k_ref, v_ref, q_ref, g_ref, q_oth, g_oth, lc_ref, s2_ref,
    st_ref, st_oth, st_lc, st_s2, bias_ref, dk_ref, dv_ref, qall, gall, stall, stat_rows,
):
    assemble(qall, q_ref, q_oth, lc_ref.at[0], s2_ref.at[0])
    assemble(gall, g_ref, g_oth, lc_ref.at[1], s2_ref.at[1])
    assemble(stall, st_ref, st_oth, st_lc, st_s2)

    def finish(at, dk, dv):
        dk_ref[:, at], dv_ref[:, at] = dk, dv

    key_sums(k_ref, v_ref, qall, gall, stall, bias_ref[...], stat_rows, finish)


def second_leg_kernel(count, *refs):
    outs = len(refs) - 4 - 3
    near_key_kernel(*refs[count:outs], *refs[outs + 1 :])
    query_kernel(*refs[:count], refs[outs])


def far_key_kernel(
    k_ref, v_ref, off_ref, st_off, bias_ref, dk_in, dv_in, dk_ref, dv_ref, stat_rows
):

    def finish(at, dk, dv):
        dk_ref[:, at] = ((dk_in[:, at] + dk) * SCALE).astype(jnp.bfloat16)
        dv_ref[:, at] = (dv_in[:, at] + dv).astype(jnp.bfloat16)

    key_sums(k_ref, v_ref, off_ref.at[0], off_ref.at[1], st_off, bias_ref[...], stat_rows, finish)


def shards(lat_count, lon_count, query, key, value, grad, pole_reach):
    rows, cols, width = query.shape
    lat, lon = lax.axis_index("lat"), lax.axis_index("lon")
    odd = lax.rem(lat, 2)
    even = odd == 0
    pair, around, across = routes(lat_count, lon_count)
    axes = ("lat", "lon")
    n_own, n_oth, n_strip, _, n_off, n_corner = pieces(rows, cols)
    near = n_own + n_oth + 2 * n_strip
    far = n_off + n_corner
    place = jnp.stack([lat, lon]).astype(jnp.int32)

    smem = pl.BlockSpec(memory_space=pltpu.SMEM)
    vmem = pl.BlockSpec(memory_space=pltpu.VMEM)

    def call(body, outs, operands, scratch=(), flops=1 << 10, scalars=False, space=pltpu.VMEM):
        return pl.pallas_call(
            body,
            out_shape=outs,
            in_specs=[smem] * scalars
            + [pl.BlockSpec(memory_space=space)] * (len(operands) - scalars),
            out_specs=jax.tree.map(lambda _: vmem, outs),
            scratch_shapes=scratch,
            compiler_params=pltpu.CompilerParams(vmem_limit_bytes=16 << 20),
            cost_estimate=pl.CostEstimate(flops=flops, bytes_accessed=1 << 20, transcendentals=0),
        )(*operands)

    def array(*shape, dtype=jnp.bfloat16):
        return jax.ShapeDtypeStruct(shape, dtype)

    f32 = jnp.float32
    heads = width // HEAD_DIM

    def strip_of(mine, other):
        side = [jnp.where(even, x[:, cols - RADIUS :], x[:, :RADIUS]) for x in (mine, other)]
        return jnp.concatenate([x.reshape(rows * RADIUS, -1) for x in side], axis=0)

    def edge_of(mine):
        return jnp.where(even, mine[:RADIUS], mine[rows - RADIUS :]).reshape(n_off, -1)

    def corner_of(first, second):
        count, half = RADIUS * RADIUS, n_strip // 2
        parts = [
            jnp.where(even, x[at : at + count], x[at + half - count : at + half])
            for x, at in ((first, 0), (second, half))
        ]
        parts.append(jnp.zeros((n_corner - 2 * count, first.shape[1]), first.dtype))
        return jnp.concatenate(parts, axis=0)

    def send(block, route):
        return lax.ppermute(block, axes, route)

    def flat(field):
        return field.reshape(n_own, field.shape[-1])

    def strips(mine, other):
        return jnp.stack([strip_of(a, b) for a, b in zip(mine, other)])

    def edges(mine):
        return jnp.stack([edge_of(a) for a in mine])

    def corners(first, second):
        return jnp.stack([corner_of(a, b) for a, b in zip(first, second)])

    key_o, value_o = send(key, pair), send(value, pair)
    query_o, grad_o = send(query, pair), send(grad, pair)
    mine = lax.optimization_barrier(jnp.stack([key, value, query, grad]))
    kv_strip = strips(mine[:2], (key_o, value_o))
    later, _ = lax.optimization_barrier((mine, kv_strip))
    kv_edge = edges(later[:2])
    kv_1 = send(kv_strip, around)
    kv_off = send(kv_edge, across)
    qg_1 = send(strips(later[2:], (query_o, grad_o)), around)
    kv_2 = send(kv_1, pair)
    kv_last = corners(kv_1, kv_2)
    kv_corner = send(kv_last, across)
    place, pole_reach, _ = lax.optimization_barrier((place, pole_reach, kv_1))
    table = np.concatenate(
        [layout(rows, cols, odd, pole) for odd in (False, True) for pole in (False, True)]
    )
    bias_near, bias_far, bias_t = call(
        functools.partial(mask_kernel, rows, cols, lat_count, lon_count),
        (
            array(n_own, near, dtype=f32),
            array(n_own, far, dtype=f32),
            array(near + far, n_own, dtype=f32),
        ),
        (place, pole_reach, jnp.asarray(table)),
        [
            pltpu.VMEM(pole_reach.shape, jnp.int32),
            pltpu.VMEM(table.shape, jnp.int32),
            pltpu.SemaphoreType.DMA((2,)),
        ],
        scalars=True,
        space=pltpu.HBM,
    )

    k, v, q, g = (flat(x) for x in mine)
    stat = array(heads, n_own, dtype=f32)
    k_near, v_near, *near_stats = call(
        near_stats_kernel,
        (array(near, width), array(near, width), stat, stat, stat),
        (q, g, k, v, flat(key_o), flat(value_o), kv_1, kv_2, bias_t),
    )
    qg_1, _ = lax.optimization_barrier((qg_1, near_stats[0]))
    qg_2 = send(qg_1, pair)
    qg_beyond = jnp.concatenate([edges(later[2:]), corners(qg_1, qg_2)], axis=1)
    near_stats[0], qg_2 = lax.optimization_barrier((near_stats[0], qg_2))
    stats, k_far, v_far = call(
        far_stats_kernel,
        (array(n_own, LANES), array(far, width), array(far, width)),
        (q, g, kv_off, kv_corner, bias_t, *near_stats),
        [pltpu.VMEM((heads, n_own), f32)] * 3,
    )
    stats_grid = stats.reshape(rows, cols, LANES)
    stats_o = send(stats_grid, pair)
    st_strip, stats_q = lax.optimization_barrier((strip_of(stats_grid, stats_o), stats))
    st_1 = send(st_strip, around)
    qg_off = send(qg_beyond, across)
    query_side = (q, g, k_near, v_near, k_far, v_far, bias_near, bias_far)
    d_query = call(query_kernel, array(n_own, first_lanes(width)), (*query_side, stats_q))
    st_1, d_query = lax.optimization_barrier((st_1, d_query))
    st_2 = send(st_1, pair)
    _, stats_q = lax.optimization_barrier((st_2, stats))
    st_off = send(
        jnp.concatenate([edge_of(stats_grid), corner_of(st_1, st_2)], axis=0), across
    )

    first_args = (*query_side, stats_q, d_query)
    d_query, d_key, d_value = call(
        functools.partial(second_leg_kernel, len(first_args)),
        (array(n_own, width), *(array(n_own, width, dtype=f32),) * 2),
        (
            *first_args,
            k, v, q, g, flat(query_o), flat(grad_o), qg_1, qg_2,
            stats, flat(stats_o), st_1, st_2, bias_near,
        ),
        [
            pltpu.VMEM((near, width), jnp.bfloat16),
            pltpu.VMEM((near, width), jnp.bfloat16),
            pltpu.VMEM((near, LANES), jnp.bfloat16),
            pltpu.VMEM((2 * heads, near), f32),
        ],
    )
    d_key, d_value = call(
        far_key_kernel,
        (array(n_own, width), array(n_own, width)),
        (k, v, qg_off, st_off, bias_far, d_key, d_value),
        [pltpu.VMEM((2 * heads, far), f32)],
    )
    shape = (rows, cols, width)
    return d_query.reshape(shape), d_key.reshape(shape), d_value.reshape(shape)


def solution(mesh):
    field = P("lat", "lon", None)
    return jax.shard_map(
        functools.partial(shards, mesh.shape["lat"], mesh.shape["lon"]),
        mesh=mesh,
        in_specs=(field, field, field, field, P()),
        out_specs=(field, field, field),
        check_vma=False,
    )
```
